128 devices in a mesh: tensor: 2 (over y_lo), dp: 4 (over y_hi, core), seq: 16 (over z, x).
Axes of the slice: x: 4, y: 4 (y_hi: 2, y_lo: 2; y = y_hi * 2 + y_lo), z: 4, core: 2. Of those that a mesh axis runs over, the one named last changes fastest.
Arguments:
- inputs: bfloat16 [4, 2048, 1024], P('dp', 'seq'), may hold values from -6 to 6
- cotangent: bfloat16 [4, 2048, 1024], P('dp', 'seq'), may hold values from -6 to 6
- norm_mix: bfloat16 [1024], replicated, may hold values from 0.5 to 1.5
- w_query: bfloat16 [1024, 1024], P(None, 'tensor'), may hold values from -0.1875 to 0.1875
- w_key: bfloat16 [1024, 1024], P(None, 'tensor'), may hold values from -0.1875 to 0.1875
- w_value: bfloat16 [1024, 2048], P(None, 'tensor'), may hold values from -0.1875 to 0.1875
- w_outgate: bfloat16 [1024, 2048], P(None, 'tensor'), may hold values from -0.1875 to 0.1875
- w_beta: bfloat16 [1024, 8], P(None, 'tensor'), may hold values from -0.1875 to 0.1875
- w_decay: bfloat16 [1024, 8], P(None, 'tensor'), may hold values from -0.1875 to 0.1875
- decay_log: bfloat16 [8], P('tensor'), may hold values from 0 to 1
- decay_bias: bfloat16 [8], P('tensor'), may hold values from -8 to -4
- conv_query: bfloat16 [1024, 4], P('tensor'), may hold values from -3 to 3
- conv_key: bfloat16 [1024, 4], P('tensor'), may hold values from -3 to 3
- conv_value: bfloat16 [2048, 4], P('tensor'), may hold values from -3 to 3
- out_gain: bfloat16 [256], replicated, may hold values from 0.5 to 1.5
- w_out: bfloat16 [2048, 1024], P('tensor'), may hold values from -0.125 to 0.125
- norm_ffn: bfloat16 [1024], replicated, may hold values from 0.5 to 1.5
- w_gate: bfloat16 [1024, 2816], P(None, 'tensor'), may hold values from -0.1875 to 0.1875
- w_up: bfloat16 [1024, 2816], P(None, 'tensor'), may hold values from -0.1875 to 0.1875
- w_down: bfloat16 [2816, 1024], P('tensor'), may hold values from -0.109375 to 0.109375
Outputs:
- output: bfloat16 [4, 2048, 1024], P('dp', 'seq')
- grad_inputs: bfloat16 [4, 2048, 1024], P('dp', 'seq')
- grad_norm_mix: bfloat16 [1024], P('seq')
- grad_w_query: bfloat16 [1024, 1024], P('seq', 'tensor')
- grad_w_key: bfloat16 [1024, 1024], P('seq', 'tensor')
- grad_w_value: bfloat16 [1024, 2048], P('seq', 'tensor')
- grad_w_outgate: bfloat16 [1024, 2048], P('seq', 'tensor')
- grad_w_beta: bfloat16 [1024, 8], P('seq', 'tensor')
- grad_w_decay: bfloat16 [1024, 8], P('seq', 'tensor')
- grad_decay_log: bfloat16 [8], P('tensor')
- grad_decay_bias: bfloat16 [8], P('tensor')
- grad_conv_query: bfloat16 [1024, 4], P(('tensor', 'seq'))
- grad_conv_key: bfloat16 [1024, 4], P(('tensor', 'seq'))
- grad_conv_value: bfloat16 [2048, 4], P(('tensor', 'seq'))
- grad_out_gain: bfloat16 [256], P('seq')
- grad_w_out: bfloat16 [2048, 1024], P(('tensor', 'seq'))
- grad_norm_ffn: bfloat16 [1024], P('seq')
- grad_w_gate: bfloat16 [1024, 2816], P('seq', 'tensor')
- grad_w_up: bfloat16 [1024, 2816], P('seq', 'tensor')
- grad_w_down: bfloat16 [2816, 1024], P(('tensor', 'seq'))
The draws below stay inside these ranges and needn't reach their ends.
All inputs are finite; a program needn't handle non-finite values.
Results may differ from the reference program's by a relative error of at most 0.025.
Values may be sent and summed in bfloat16 or wider, within the bound.
No kernel may reach another device: no remote copies, remote signals or barrier semaphores. Data moves between devices by JAX's collectives and lax.ppermute only.
A program may use at most 128 MiB of HBM per device.

```python
import jax
import jax.numpy as jnp
from jax import lax

D = 1024
HEADS = 8
DK = 128
DV = 256
FF = 2816
KW = 4
GROUP = 64
SEQ_LEN = 2048
SEQS = 4


def block_levels(rng, shape, pieces, least, high):
    level, own = 1.0, jax.random.fold_in(rng, 6)
    for axis_at, blocks in pieces:
        steps = jnp.exp(jax.random.uniform(jax.random.fold_in(own, axis_at), (blocks,), jnp.float32, least / len(pieces), high / len(pieces)))
        level = level * jnp.repeat(steps, shape[axis_at] // blocks).reshape([-1 if axis == axis_at else 1 for axis in range(len(shape))])
    return level


def normal_values(key, extent, scale, bound, pieces=(), kind=jnp.bfloat16):
    loudness = block_levels(key, extent, pieces, -0.22, 0.18) if pieces else 1.0
    array = jax.random.normal(key, extent, jnp.float32) * scale * loudness
    return jnp.minimum(jnp.maximum(array, -bound), bound).astype(kind)


def setup_inputs(seed: int = 0) -> dict:
    arg_keys = jax.random.split(jax.random.key(seed), 21)
    return {
        "inputs": normal_values(arg_keys[0], (SEQS, SEQ_LEN, D), 1.0, 6.0, ((0, 4), (1, 16))),
        "cotangent": normal_values(arg_keys[1], (SEQS, SEQ_LEN, D), 1.0, 6.0, ((0, 4), (1, 16))),
        "norm_mix": jnp.clip(1.0 + 0.1 * jax.random.normal(arg_keys[2], (D,), jnp.float32), 0.5, 1.5).astype(jnp.bfloat16),
        "w_query": normal_values(arg_keys[3], (D, HEADS * DK), D ** -0.5, 0.1875, ((1, 2),)),
        "w_key": normal_values(arg_keys[4], (D, HEADS * DK), D ** -0.5, 0.1875, ((1, 2),)),
        "w_value": normal_values(arg_keys[5], (D, HEADS * DV), D ** -0.5, 0.1875, ((1, 2),)),
        "w_outgate": normal_values(arg_keys[6], (D, HEADS * DV), D ** -0.5, 0.1875, ((1, 2),)),
        "w_beta": normal_values(arg_keys[7], (D, HEADS), D ** -0.5, 0.1875, ((1, 2),)),
        "w_decay": normal_values(arg_keys[8], (D, HEADS), D ** -0.5, 0.1875, ((1, 2),)),
        "decay_log": jnp.clip(1.0 * jax.random.uniform(arg_keys[9], (HEADS,), jnp.float32) ** block_levels(arg_keys[9], (HEADS,), ((0, 2),), -0.2, 0.2), 0.0, 1.0).astype(jnp.bfloat16),
        "decay_bias": jnp.clip(-8.0 + 4.0 * jax.random.uniform(arg_keys[10], (HEADS,), jnp.float32) ** block_levels(arg_keys[10], (HEADS,), ((0, 2),), -0.2, 0.2), -8.0, -4.0).astype(jnp.bfloat16),
        "conv_query": normal_values(arg_keys[11], (HEADS * DK, KW), KW ** -0.5, 3.0, ((0, 2),)),
        "conv_key": normal_values(arg_keys[12], (HEADS * DK, KW), KW ** -0.5, 3.0, ((0, 2),)),
        "conv_value": normal_values(arg_keys[13], (HEADS * DV, KW), KW ** -0.5, 3.0, ((0, 2),)),
        "out_gain": jnp.clip(1.0 + 0.1 * jax.random.normal(arg_keys[14], (DV,), jnp.float32), 0.5, 1.5).astype(jnp.bfloat16),
        "w_out": normal_values(arg_keys[15], (HEADS * DV, D), (HEADS * DV) ** -0.5, 0.125, ((0, 2),)),
        "norm_ffn": jnp.clip(1.0 + 0.1 * jax.random.normal(arg_keys[16], (D,), jnp.float32), 0.5, 1.5).astype(jnp.bfloat16),
        "w_gate": normal_values(arg_keys[17], (D, FF), D ** -0.5, 0.1875, ((1, 2),)),
        "w_up": normal_values(arg_keys[18], (D, FF), D ** -0.5, 0.1875, ((1, 2),)),
        "w_down": normal_values(arg_keys[19], (FF, D), FF ** -0.5, 0.109375, ((0, 2),)),
    }


@jax.custom_vjp
def low(v):
    return lax.optimization_barrier(v.astype(jnp.bfloat16)).astype(jnp.float32)

@jax.custom_vjp
def low_back(v):
    return v

def low_keep(v):
    return (low(v), None)

def low_pass(kept, grad):
    return (grad,)

def back_keep(v):
    return (v, None)

def back_low(kept, grad):
    return (low(grad),)
low.defvjp(low_keep, low_pass)
low_back.defvjp(back_keep, back_low)
highest = lax.Precision.HIGHEST
epsilon = 1e-05
smallest = 1e-06

def product(left_op, right_op):
    return jnp.dot(left_op, right_op, precision=highest)

def rms_rows(values, scales):
    return values * lax.rsqrt(lax.optimization_barrier(jnp.mean(values * values, axis=-1, keepdims=True)) + epsilon) * scales

def unit_heads(values):
    return values * lax.rsqrt(lax.optimization_barrier(jnp.sum(values * values, axis=-1, keepdims=True)) + smallest)

def short_conv(values, filters):
    length = values.shape[0]
    padded = jnp.pad(values, ((KW - 1, 0), (0, 0)))
    summed = padded[0:length] * filters[:, 0]
    for offset in range(1, KW):
        summed = summed + padded[offset:offset + length] * filters[:, offset]
    return jax.nn.silu(summed)

def token_step(carried, current):
    query_now, key_now, value_now, beta_now, decay_now = current
    faded = jnp.exp(decay_now)[:, None, None] * carried
    recalled = jnp.einsum('hd,hdw->hw', key_now, faded, precision=highest)
    updated = faded + (beta_now[:, None] * key_now)[:, :, None] * (value_now - recalled)[:, None, :]
    return (updated, jnp.einsum('hd,hdw->hw', query_now, updated, precision=highest))

def block_step(carried, block_in):
    return lax.scan(token_step, carried, block_in)

def delta_tokens(queries, keys_in, values, beta_rows, decays):
    length = queries.shape[0]
    blocks = length // GROUP
    shaped = tuple((array_in.reshape((blocks, GROUP) + array_in.shape[1:]) for array_in in (queries, keys_in, values, beta_rows, decays)))
    start_state = jnp.zeros((HEADS, DK, DV), jnp.float32)
    result = lax.scan(jax.checkpoint(block_step), start_state, shaped)
    return result[1].reshape(length, HEADS, DV)

def block_layer(params, seq_in):
    norm_mix, w_query, w_key, w_value, w_outgate, w_beta, w_decay, decay_log, decay_bias, conv_query, conv_key, conv_value, out_gain, w_out, norm_ffn, w_gate, w_up, w_down = params
    length = seq_in.shape[0]
    normed = low(rms_rows(seq_in, norm_mix))
    query_pre = low_back(low(product(normed, w_query)))
    key_pre = low_back(low(product(normed, w_key)))
    value_pre = low_back(low(product(normed, w_value)))
    queries = low(unit_heads(short_conv(query_pre, conv_query).reshape(length, HEADS, DK)) * DK ** (-0.5))
    keys_in = low(unit_heads(short_conv(key_pre, conv_key).reshape(length, HEADS, DK)))
    values = low(short_conv(value_pre, conv_value).reshape(length, HEADS, DV))
    beta_rows = jax.nn.sigmoid(low_back(product(normed, w_beta)))
    decays = -jnp.exp(decay_log) * jax.nn.softplus(low_back(product(normed, w_decay)) + decay_bias)
    mixed = delta_tokens(queries, keys_in, values, beta_rows, decays)
    gate_pre = low_back(product(normed, w_outgate)).reshape(length, HEADS, DV)
    gated = mixed * lax.rsqrt(lax.optimization_barrier(jnp.mean(mixed * mixed, axis=-1, keepdims=True)) + epsilon) * out_gain * jax.nn.silu(gate_pre)
    branch = low_back(product(low(gated.reshape(length, HEADS * DV)), w_out))
    middle = seq_in + branch
    normed_two = low(rms_rows(middle, norm_ffn))
    gate_ffn = low_back(product(normed_two, w_gate))
    up_ffn = low_back(product(normed_two, w_up))
    hidden = low(jax.nn.silu(gate_ffn) * up_ffn)
    return middle + low_back(product(hidden, w_down))

def reference(inputs, cotangent, norm_mix, w_query, w_key, w_value, w_outgate, w_beta, w_decay, decay_log, decay_bias, conv_query, conv_key, conv_value, out_gain, w_out, norm_ffn, w_gate, w_up, w_down):
    params = tuple((weight.astype(jnp.float32) for weight in (norm_mix, w_query, w_key, w_value, w_outgate, w_beta, w_decay, decay_log, decay_bias, conv_query, conv_key, conv_value, out_gain, w_out, norm_ffn, w_gate, w_up, w_down)))

    def one_sequence(totals, seq_pair):
        seq_in, seq_cot = seq_pair
        outputs, pullback = jax.vjp(block_layer, params, seq_in)
        grad_tree, grad_seq = pullback(seq_cot)
        totals = tuple((running + added for running, added in zip(totals, grad_tree)))
        return (totals, (outputs, grad_seq))
    zeros = tuple((jnp.zeros_like(weight) for weight in params))
    totals, (outputs, grad_seqs) = lax.scan(one_sequence, zeros, (inputs.astype(jnp.float32), cotangent.astype(jnp.float32)))
    totals = tuple((running.astype(jnp.bfloat16) for running in totals))
    return (outputs.astype(jnp.bfloat16), grad_seqs.astype(jnp.bfloat16), totals[0], totals[1], totals[2], totals[3], totals[4], totals[5], totals[6], totals[7], totals[8], totals[9], totals[10], totals[11], totals[12], totals[13], totals[14], totals[15], totals[16], totals[17])
```

```python
import functools

import jax
import jax.numpy as jnp
from jax import lax
from jax.experimental import pallas as pl
from jax.experimental.pallas import tpu as pltpu
from jax.sharding import PartitionSpec as P

f32 = jnp.float32
bf16 = jnp.bfloat16
epsilon = 1e-05
smallest = 1e-06
TOK = 128
HEADS = 4
DK = 128
DV = 256
QK = HEADS * DK
VW = HEADS * DV
PRE = 2 * QK + VW
SEQ = 16
HALO = 16
MIB = 1024 * 1024


def kernel_call(body, outs, *args, scratch=(), limit=40 * MIB, flops=0, moved=0):
    out_shape = [jax.ShapeDtypeStruct(shape, kind) for shape, kind in outs]
    if not moved:
        moved = sum(a.size * a.dtype.itemsize for a in args)
        moved += sum(o.size * o.dtype.itemsize for o in out_shape)
    return pl.pallas_call(
        body,
        out_shape=out_shape,
        in_specs=[pl.BlockSpec(memory_space=pltpu.VMEM)] * len(args),
        out_specs=[pl.BlockSpec(memory_space=pltpu.VMEM)] * len(outs),
        scratch_shapes=list(scratch),
        compiler_params=pltpu.CompilerParams(vmem_limit_bytes=limit),
        cost_estimate=pl.CostEstimate(flops=flops, bytes_accessed=moved, transcendentals=0),
    )(*args)


def mm(a, b):
    return jnp.dot(a.astype(bf16), b.astype(bf16), preferred_element_type=f32)


def mt(a, b):
    return lax.dot_general(
        a.astype(bf16), b.astype(bf16), (((1,), (1,)), ((), ())), preferred_element_type=f32
    )


def tm(a, b):
    return lax.dot_general(
        a.astype(bf16), b.astype(bf16), (((0,), (0,)), ((), ())), preferred_element_type=f32
    )


def halves(a):
    high = a.astype(bf16)
    return high, (a - high.astype(f32)).astype(bf16)


def mm3(a, b):
    ah, al = halves(a)
    bh, bl = halves(b)
    return mm(jnp.concatenate([ah, al, ah], axis=1), jnp.concatenate([bh, bh, bl], axis=0))


def mm2(a, b):
    ah, al = halves(a)
    return mm(jnp.concatenate([ah, al], axis=1), jnp.concatenate([b, b], axis=0))


def thirds(a):
    high = a.astype(bf16)
    rest = a - high.astype(f32)
    mid = rest.astype(bf16)
    return high, mid, (rest - mid.astype(f32)).astype(bf16)


def masks():
    rows = lax.broadcasted_iota(jnp.int32, (TOK, TOK), 0)
    cols = lax.broadcasted_iota(jnp.int32, (TOK, TOK), 1)
    return rows, cols


def sigmoid(v):
    return 1.0 / (1.0 + jnp.exp(-v))


def fading_of(c_col, c_row, inclusive):
    return jnp.where(inclusive, jnp.exp(jnp.where(inclusive, c_col - c_row, 0.0)), 0.0)


def front_kernel(
    pre, halo, filt, bdv, z_o, q_o, k_o, x_o, c_o, uv_o, uk_o, ol_o, qe_o, send_o, ext
):
    ext[0:HALO] = halo[...].astype(f32)
    ext[HALO:] = pre[...].astype(f32)

    def activated(at, width):
        z = ext[pl.ds(HALO - 3, TOK), at : at + width] * filt[0:1, at : at + width]
        for j in range(1, 4):
            z = z + ext[pl.ds(HALO - 3 + j, TOK), at : at + width] * filt[j : j + 1, at : at + width]
        z_o[:, at : at + width] = z
        return z * sigmoid(z)

    rows, cols = masks()
    inclusive = rows >= cols
    strict = rows > cols
    lower = jnp.where(inclusive, 1.0, 0.0).astype(bf16)
    eye = jnp.where(rows == cols, 1.0, 0.0)
    scal = bdv[...]
    c_all = mm(
        jnp.concatenate([lower, lower, lower], axis=1), jnp.concatenate(thirds(scal), axis=0)
    )
    c_o[...] = c_all
    c_t = c_all.T
    b_t = scal.T
    for h in range(HEADS):
        a_q = activated(h * DK, DK)
        a_k = activated(QK + h * DK, DK)
        a_v = activated(2 * QK + h * DV, DV)
        q = (
            a_q
            * lax.rsqrt(jnp.sum(a_q * a_q, axis=1, keepdims=True) + smallest)
            * DK ** (-0.5)
        ).astype(bf16)
        k = (a_k * lax.rsqrt(jnp.sum(a_k * a_k, axis=1, keepdims=True) + smallest)).astype(bf16)
        v = a_v.astype(bf16)
        q_o[:, h * DK : (h + 1) * DK] = q
        k_o[:, h * DK : (h + 1) * DK] = k
        c_col = c_all[:, HEADS + h : HEADS + h + 1]
        c_row = c_t[HEADS + h : HEADS + h + 1, :]
        b_col = scal[:, h : h + 1]
        b_row = b_t[h : h + 1, :]
        fading = fading_of(c_col, c_row, inclusive)
        low = jnp.where(strict, fading * b_row * mt(k, k), 0.0)
        inv = eye - jnp.where((rows // 2 == cols // 2) & strict, low, 0.0)
        size = 2
        while size < TOK:
            part = (
                (rows // (2 * size) == cols // (2 * size))
                & (rows // size % 2 == 1)
                & (cols // size % 2 == 0)
            )
            inv = inv - mm3(inv, mm3(jnp.where(part, low, 0.0), inv))
            size *= 2
        x_o[h] = inv
        growth = jnp.exp(c_col)
        u_v = mm2(inv, v)
        u_k = mm2(inv * jnp.exp(c_row), k)
        uv_o[:, h * DV : (h + 1) * DV] = u_v
        uk_o[:, h * DK : (h + 1) * DK] = u_k.astype(bf16)
        scores = fading * mt(q, k) * b_row
        ol_o[:, h * DV : (h + 1) * DV] = mm(scores, u_v)
        qe_o[:, h * DK : (h + 1) * DK] = (growth * q.astype(f32) - mm(scores, u_k)).astype(bf16)
        c_last = c_all[TOK - 1 : TOK, HEADS + h : HEADS + h + 1]
        b_k = b_col * jnp.exp(c_last - c_col) * k.astype(f32)
        turned = (eye * jnp.exp(c_last) - tm(u_k, b_k)).astype(bf16)
        offset = tm(u_v, b_k).astype(bf16)
        for g in range(4):
            send_o[h * 4 + g, 0:DK] = turned
            send_o[h * 4 + g, DK : DK + 64] = offset[64 * g : 64 * g + 64]


def scan_kernel(maps, out):
    state = jnp.zeros((64, DK), f32)
    for d in range(SEQ):
        out[d] = state.astype(bf16)
        if d < SEQ - 1:
            turned = maps[d, 0:DK]
            state = mm(
                jnp.concatenate(halves(state), axis=1), jnp.concatenate([turned, turned], axis=0)
            ) + maps[d, DK : DK + 64].astype(f32)


def scan_back_kernel(grads, maps, out):
    state = jnp.zeros((64, DK), f32)
    for d in range(SEQ - 1, -1, -1):
        out[d] = state.astype(bf16)
        if d > 0:
            turned = maps[d, 0:DK]
            state = mt(
                jnp.concatenate(halves(state), axis=1), jnp.concatenate([turned, turned], axis=1)
            ) + grads[d].astype(f32)


def mixed_kernel(ol, qe, st, gate_pre, gain, mixed_o, gated_o):
    for h in range(HEADS):
        at = slice(h * DV, (h + 1) * DV)
        state = st[4 * h : 4 * h + 4].reshape(DV, DK)
        mixed = ol[:, at] + mt(qe[:, h * DK : (h + 1) * DK], state)
        mixed_o[:, at] = mixed
        normed = mixed * lax.rsqrt(jnp.mean(mixed * mixed, axis=1, keepdims=True) + epsilon)
        gate = gate_pre[:, at]
        gated_o[:, at] = (normed * gain[...] * (gate * sigmoid(gate))).astype(bf16)


def mixed_back_kernel(gated_grad, mixed_in, gate_pre, gain, qe, do_o, gp_o, gain_o, sg_o):
    gain_total = jnp.zeros((1, DV), f32)
    for h in range(HEADS):
        at = slice(h * DV, (h + 1) * DV)
        mixed = mixed_in[:, at]
        root = lax.rsqrt(jnp.mean(mixed * mixed, axis=1, keepdims=True) + epsilon)
        m = mixed * root
        gate = gate_pre[:, at]
        sig = sigmoid(gate)
        grad = gated_grad[:, at]
        gm = grad * m
        silu = gate * sig
        gain_total = gain_total + jnp.sum(gm * silu, axis=0, keepdims=True)
        gp_o[:, at] = (gm * gain[...] * (sig * (1.0 + gate * (1.0 - sig)))).astype(bf16)
        e = grad * gain[...] * silu
        d_out = (root * (e - m * jnp.mean(e * m, axis=1, keepdims=True))).astype(bf16)
        do_o[:, at] = d_out
        sg = tm(d_out, qe[:, h * DK : (h + 1) * DK])
        sg_o[4 * h : 4 * h + 4] = sg.astype(bf16).reshape(4, 64, DK)
    gain_o[...] = gain_total


def back_kernel(
    pre, halo, filt, bdv, z_i, q_i, k_i, x_i, c_i, uv_i, uk_i, do_i, st_i, gt_i,
    dz_o, dzh_o, fg_o, dbd_o, ext,
):
    ext[0:HALO] = halo[...].astype(f32)
    ext[HALO:] = pre[...].astype(f32)
    rows, cols = masks()
    inclusive = rows >= cols
    strict = rows > cols
    scal = bdv[...]
    c_all = c_i[...]
    c_t = c_all.T
    b_t = scal.T

    def finish(grad, z, sig, at, width):
        dz = grad * (sig * (1.0 + z * (1.0 - sig)))
        dz_o[:, at : at + width] = dz
        dzh_o[:, at : at + width] = dz[0:HALO].astype(bf16)
        for j in range(4):
            fg_o[j : j + 1, at : at + width] = jnp.sum(
                dz * ext[pl.ds(HALO - 3 + j, TOK), at : at + width], axis=0, keepdims=True
            )

    fg_o[4:8, :] = jnp.zeros((4, PRE), f32)
    lane = lax.broadcasted_iota(jnp.int32, (TOK, TOK), 1)
    cols_acc = jnp.zeros((TOK, TOK), f32)
    sub = lax.broadcasted_iota(jnp.int32, (TOK, TOK), 0)
    rows_acc = jnp.zeros((TOK, TOK), f32)
    for h in range(HEADS):
        atv = slice(h * DV, (h + 1) * DV)
        atk = slice(h * DK, (h + 1) * DK)
        q = q_i[:, atk]
        k = k_i[:, atk]
        q32 = q.astype(f32)
        k32 = k.astype(f32)
        st = st_i[4 * h : 4 * h + 4].reshape(DV, DK)
        gt = gt_i[4 * h : 4 * h + 4].reshape(DV, DK)
        d_out = do_i[:, atv]
        c_col = c_all[:, HEADS + h : HEADS + h + 1]
        c_row = c_t[HEADS + h : HEADS + h + 1, :]
        c_last = c_all[TOK - 1 : TOK, HEADS + h : HEADS + h + 1]
        b_col = scal[:, h : h + 1]
        b_row = b_t[h : h + 1, :]
        fading = fading_of(c_col, c_row, inclusive)
        growth = jnp.exp(c_col)
        remains = jnp.exp(c_last - c_col)
        scores = fading * mt(q, k)
        low_one = jnp.where(strict, fading * mt(k, k), 0.0)
        u = uv_i[:, atv] - mt(uk_i[:, atk], st)
        w = (b_col * u).astype(bf16)
        k_rem = remains * k32
        d_w = tm(scores, d_out) + mt(k_rem, gt)
        d_beta = jnp.sum(u * d_w, axis=1, keepdims=True)
        d_r = tm(x_i[h], b_col * d_w)
        d_rl = d_r.astype(bf16)
        d_low = jnp.where(strict, -mt(d_rl, u), 0.0)
        d_a = jnp.where(inclusive, mt(d_out, w), 0.0)
        d_qk = d_a * fading
        e_beta = d_low * low_one
        e_sum = d_a * scores + e_beta * b_row
        d_kk = d_low * fading * b_row
        d_os = mm(d_out, st)
        d_rs = mm(d_rl, st)
        w_g = mm(w, gt)
        dq = mm(d_qk, k) + growth * d_os
        dk = tm(d_qk, q) + mm(d_kk, k) + tm(d_kk, k) - growth * d_rs + remains * w_g
        rem_sum = jnp.sum(k_rem * w_g, axis=1, keepdims=True)
        d_c = (
            jnp.sum(e_sum, axis=1, keepdims=True)
            + growth * jnp.sum(q32 * d_os - k32 * d_rs, axis=1, keepdims=True)
            - rem_sum
        )
        last = jnp.sum(rem_sum, axis=0, keepdims=True) + jnp.exp(c_last) * jnp.sum(
            jnp.sum(st.astype(f32) * gt.astype(f32), axis=1, keepdims=True), axis=0, keepdims=True
        )
        d_c = d_c + jnp.where(sub[:, 0:1] == TOK - 1, last, 0.0)
        cols_acc = cols_acc + jnp.where(lane == h, d_beta, 0.0)
        cols_acc = cols_acc + jnp.where(lane == HEADS + h, d_c, 0.0)
        rows_acc = rows_acc + jnp.where(sub == h, jnp.sum(e_beta, axis=0, keepdims=True), 0.0)
        rows_acc = rows_acc - jnp.where(
            sub == HEADS + h, jnp.sum(e_sum, axis=0, keepdims=True), 0.0
        )
        for grad, base, scale in ((dq, 0, DK ** (-0.5)), (dk, QK, 1.0)):
            at = base + h * DK
            z = z_i[:, at : at + DK]
            sig = sigmoid(z)
            act = z * sig
            root = lax.rsqrt(jnp.sum(act * act, axis=1, keepdims=True) + smallest)
            unit = act * root
            grad = grad * scale
            d_act = root * (grad - unit * jnp.sum(unit * grad, axis=1, keepdims=True))
            finish(d_act, z, sig, at, DK)
        at = 2 * QK + h * DV
        z = z_i[:, at : at + DV]
        finish(d_r, z, sigmoid(z), at, DV)
    total = cols_acc + rows_acc.T
    upper = jnp.where(rows <= cols, 1.0, 0.0).astype(bf16)
    summed = mm(
        jnp.concatenate([upper, upper, upper], axis=1), jnp.concatenate(thirds(total), axis=0)
    )
    dbd_o[...] = jnp.where(lane < HEADS, total, summed)


def conv_back_kernel(dz, after, filt, pre_o, ext):
    ext[0:TOK] = dz[...]
    ext[TOK:] = after[...].astype(f32)
    for at in range(0, PRE, 256):
        total = ext[pl.ds(3, TOK), at : at + 256] * filt[0:1, at : at + 256]
        for j in range(1, 4):
            total = total + ext[pl.ds(3 - j, TOK), at : at + 256] * filt[j : j + 1, at : at + 256]
        pre_o[:, at : at + 256] = total.astype(bf16)


def padded_rows(left):
    return -(-(left.shape[1] // SEQ) // 16) * 16


def pieces_rows(pieces):
    return sum(padded_rows(left) * (right.shape[1] // 128) for left, right in pieces)


def weight_body(count, added, refs):
    ins = refs[: 2 * count]
    adds = refs[2 * count : 2 * count + added]
    out = refs[2 * count + added]
    turned = refs[2 * count + added + 1]
    offset = 0
    part = 0
    done = 0
    for at in range(count):
        left, right = ins[2 * at], ins[2 * at + 1]
        width = left.shape[1]
        rows = width // SEQ
        padded = padded_rows(left)
        turned[0:width] = left[...].T

        def tile(n, carry, right=right, width=width, rows=rows, padded=padded, offset=offset,
                 part=part, done=done):
            piece = jnp.dot(
                turned[0:width],
                right[:, pl.ds(pl.multiple_of(n * 128, 128), 128)],
                preferred_element_type=f32,
            ).reshape(SEQ, rows, 128)
            if padded > rows:
                piece = jnp.concatenate([piece, jnp.zeros((SEQ, padded - rows, 128), f32)], axis=1)
            if added:
                where = pl.ds(pl.multiple_of(offset - done + n * padded, 16), padded)
                piece = piece + adds[part][:, where].astype(f32)
            where = pl.ds(pl.multiple_of(offset + n * padded, 16), padded)
            out[:, where] = piece.astype(bf16)
            return carry

        lax.fori_loop(0, right.shape[1] // 128, tile, 0)
        offset += padded * (right.shape[1] // 128)
        if added and offset - done == adds[part].shape[1]:
            done = offset
            part += 1


def weight_grads(pieces, adds=()):
    total = pieces_rows(pieces)
    args = [operand for pair in pieces for operand in pair] + list(adds)

    def body(*refs):
        weight_body(len(pieces), len(adds), refs)

    return kernel_call(
        body,
        [((SEQ, total, 128), bf16)],
        *args,
        scratch=[pltpu.VMEM((1408, TOK), bf16)],
        limit=48 * MIB,
        flops=2 * 128 * 128 * SEQ * total,
    )[0]


SPLIT = 272


def spread_body(place, kept, small, small_in, *outs):
    rows = kept.shape[1]
    z_at, x_at = place[0], place[1]
    for s in range(4):
        x_to = lax.rem(x_at + s, 4)
        z_to = lax.rem(z_at + s, 4)
        for other in range(4):
            outs[s][other] = kept[other * 4 + x_to, 0:SPLIT]
            outs[4 + s][other, 0 : rows - SPLIT] = kept[z_to * 4 + other, SPLIT:rows]
            outs[4 + s][other, rows - SPLIT :] = (
                small[z_to * 4 + other].astype(f32) + small_in[z_to * 4 + other].astype(f32)
            ).astype(bf16)


def spread_again_body(place, *refs):
    z_at, x_at = place[0], place[1]
    first, second, outs = refs[0:4], refs[4:8], refs[8:]
    rows = second[0].shape[1]
    for s in range(4):
        z_to = lax.rem(z_at + s, 4)
        x_to = lax.rem(x_at + s, 4)
        total = first[0][z_to].astype(f32)
        other = second[0][x_to].astype(f32)
        for n in range(1, 4):
            total = total + first[n][z_to].astype(f32)
            other = other + second[n][x_to].astype(f32)
        outs[s][...] = total.astype(bf16)
        outs[4 + s][...] = other.astype(bf16)
        outs[4 + s][rows - 16 :] = in_order(
            [second[n][x_to, rows - 16 : rows] for n in range(4)], z_at
        ).astype(bf16)


def in_order(terms, own):
    total = None
    for source in range(4):
        which = lax.rem(own + 4 - source, 4)
        term = jnp.zeros(terms[0].shape, f32)
        for n in range(4):
            term = jnp.where(which == n, terms[n].astype(f32), term)
        total = term if total is None else total + term
    return total


def gather_body(place, *refs):
    out = refs[8]
    rows = out.shape[0]
    total = refs[0][...].astype(f32)
    other = refs[4][...].astype(f32)
    for n in range(1, 4):
        total = total + refs[n][...].astype(f32)
        other = other + refs[4 + n][...].astype(f32)
    out[0:SPLIT] = total.astype(bf16)
    out[SPLIT:] = other.astype(bf16)
    out[rows - 16 :] = in_order(
        [refs[4 + n][rows - SPLIT - 16 : rows - SPLIT] for n in range(4)], place[1]
    ).astype(bf16)


def placed_call(body, outs, place, *args):
    out_shape = [jax.ShapeDtypeStruct(shape, bf16) for shape in outs]
    return pl.pallas_call(
        body,
        out_shape=out_shape,
        in_specs=[pl.BlockSpec(memory_space=pltpu.SMEM)]
        + [pl.BlockSpec(memory_space=pltpu.VMEM)] * len(args),
        out_specs=[pl.BlockSpec(memory_space=pltpu.VMEM)] * len(outs),
        compiler_params=pltpu.CompilerParams(vmem_limit_bytes=40 * MIB),
    )(place, *args)


def along_x(steps):
    return [(z * 4 + x, z * 4 + (x + steps) % 4) for z in range(4) for x in range(4)]


def along_z(steps):
    return [(z * 4 + x, (z + steps) % 4 * 4 + x) for z in range(4) for x in range(4)]


def swap_tensor(value):
    return lax.ppermute(value, "tensor", [(0, 1), (1, 0)])


def swap_core(value):
    return lax.ppermute(value, "dp", [(0, 1), (1, 0), (2, 3), (3, 2)])


def swap_far(value):
    return lax.ppermute(value, "dp", [(0, 2), (2, 0), (1, 3), (3, 1)])


def shift(value, steps):
    first, last = max(0, -steps), min(SEQ, SEQ - steps)
    return lax.ppermute(value, "seq", [(at, at + steps) for at in range(first, last)])


def exchange(value):
    return lax.all_to_all(value, "seq", 0, 0, tiled=True)


def over_dp(shared):
    mine = (shared.astype(f32) + swap_far(shared).astype(f32)).astype(bf16)
    other = swap_core(mine)
    first = lax.axis_index("dp") % 2 == 0
    return jnp.where(first, mine, other), jnp.where(first, other, mine)


def tiles_to_rows(block, rows, padded):
    tiles = block.shape[0] // padded
    return (
        block.reshape(tiles, padded, 128)[:, :rows].transpose(1, 0, 2).reshape(rows, tiles * 128)
    )


def dot(a, b):
    return jnp.dot(a, b, preferred_element_type=f32)


def dot_t(a, b):
    return lax.dot_general(a, b, (((1,), (1,)), ((), ())), preferred_element_type=f32)


def norm_parts(values):
    root = lax.rsqrt(jnp.mean(values * values, axis=-1, keepdims=True) + epsilon)
    return root, values * root


def norm_back(grad, gain, root, unit):
    e = grad * gain
    return root * (e - unit * jnp.mean(e * unit, axis=-1, keepdims=True))


def per_device(
    inputs,
    cotangent,
    norm_mix,
    w_query,
    w_key,
    w_value,
    w_outgate,
    w_beta,
    w_decay,
    decay_log,
    decay_bias,
    conv_query,
    conv_key,
    conv_value,
    out_gain,
    w_out,
    norm_ffn,
    w_gate,
    w_up,
    w_down,
):
    width = inputs.shape[2]
    first = lax.axis_index("dp") % 2 == 0
    at = lax.axis_index("seq")
    place = jnp.stack([at // 4, at % 4]).astype(jnp.int32)
    residual = inputs.reshape(TOK, width).astype(f32)
    feed_grad = cotangent.reshape(TOK, width)
    gain_mix = norm_mix.astype(f32)
    gain_ffn = norm_ffn.astype(f32)
    gain_head = out_gain.astype(f32).reshape(1, DV)
    filters = jnp.concatenate([conv_query, conv_key, conv_value], axis=0).astype(f32)
    filt = jnp.pad(filters.T, ((0, 4), (0, 0)))

    root_mix, unit_mix = norm_parts(residual)
    normed_low = (unit_mix * gain_mix).astype(bf16)
    mixed_pre = jnp.concatenate(
        [dot(normed_low, w_query), dot(normed_low, w_key), dot(normed_low, w_value)], axis=1
    ).astype(bf16)
    halo = shift(mixed_pre[TOK - HALO :], 1)
    beta_rows = jax.nn.sigmoid(dot(normed_low, w_beta))
    decay_at = dot(normed_low, w_decay) + decay_bias.astype(f32)
    decay_rate = -jnp.exp(decay_log.astype(f32))
    decays = decay_rate * jax.nn.softplus(decay_at)
    bdv = jnp.pad(jnp.concatenate([beta_rows, decays], axis=1), ((0, 0), (0, 120)))
    gate_pre = dot(normed_low, w_outgate)

    z, q, k, inverse, c_all, u_v, u_k, out_local, q_eff, maps = kernel_call(
        front_kernel,
        [
            ((TOK, PRE), f32),
            ((TOK, QK), bf16),
            ((TOK, QK), bf16),
            ((HEADS, TOK, TOK), f32),
            ((TOK, TOK), f32),
            ((TOK, VW), f32),
            ((TOK, QK), bf16),
            ((TOK, VW), f32),
            ((TOK, QK), bf16),
            ((SEQ, DK + 64, DK), bf16),
        ],
        mixed_pre,
        halo,
        filt,
        bdv,
        scratch=[pltpu.VMEM((TOK + HALO, PRE), f32)],
    )
    maps = exchange(maps)
    (states,) = kernel_call(scan_kernel, [((SEQ, 64, DK), bf16)], maps)
    states = exchange(states)
    mixed, gated_low = kernel_call(
        mixed_kernel,
        [((TOK, VW), f32), ((TOK, VW), bf16)],
        out_local,
        q_eff,
        states,
        gate_pre,
        gain_head,
    )
    branch = dot(gated_low, w_out).astype(bf16)
    branch_in = swap_tensor(branch)
    hidden_grad = dot_t(feed_grad, w_down)
    middle = residual + (branch.astype(f32) + branch_in.astype(f32))
    root_ffn, unit_ffn = norm_parts(middle)
    two_low = (unit_ffn * gain_ffn).astype(bf16)
    gate_ffn = dot(two_low, w_gate)
    up_ffn = dot(two_low, w_up)
    sig = jax.nn.sigmoid(gate_ffn)
    silu = gate_ffn * sig
    hidden_low = (silu * up_ffn).astype(bf16)
    gate_low = (hidden_grad * up_ffn * (sig * (1.0 + gate_ffn * (1.0 - sig)))).astype(bf16)
    up_low = (hidden_grad * silu).astype(bf16)
    two_part = (dot_t(gate_low, w_gate) + dot_t(up_low, w_up)).astype(bf16)
    two_in = swap_tensor(two_part)
    feed_part = dot(hidden_low, w_down).astype(bf16)
    feed_in = swap_tensor(feed_part)
    output = (middle + (feed_part.astype(f32) + feed_in.astype(f32))).astype(bf16)

    half = width // 2
    ffn_sent = weight_grads(
        [
            (two_low, jnp.where(first, up_low, gate_low)),
            (hidden_low, jnp.where(first, feed_grad[:, half:], feed_grad[:, :half])),
        ]
    )
    ffn_in = swap_core(ffn_sent)

    two_grad = two_part.astype(f32) + two_in.astype(f32)
    grad_norm_ffn = jnp.sum(two_grad * unit_ffn, axis=0)
    middle_grad = feed_grad.astype(f32) + norm_back(two_grad, gain_ffn, root_ffn, unit_ffn)
    branch_low = middle_grad.astype(bf16)
    gated_grad = dot_t(branch_low, w_out)
    mixed_grad, gate_pre_low, gain_grad, start_grad = kernel_call(
        mixed_back_kernel,
        [((TOK, VW), bf16), ((TOK, VW), bf16), ((1, DV), f32), ((SEQ, 64, DK), bf16)],
        gated_grad,
        mixed,
        gate_pre,
        gain_head,
        q_eff,
    )
    out_sent = weight_grads(
        [
            (
                jnp.where(first, gated_low, normed_low),
                jnp.where(first, branch_low, gate_pre_low),
            )
        ]
    )
    out_in = swap_core(out_sent)
    early = weight_grads(
        [
            (two_low, jnp.where(first, gate_low, up_low)),
            (hidden_low, jnp.where(first, feed_grad[:, :half], feed_grad[:, half:])),
            (
                jnp.where(first, normed_low, gated_low),
                jnp.where(first, gate_pre_low, branch_low),
            ),
        ],
        [ffn_in, out_in],
    )
    early = lax.psum_scatter(early, "seq", scatter_dimension=0, tiled=True)

    start_grad = exchange(start_grad)
    (end_grads,) = kernel_call(scan_back_kernel, [((SEQ, 64, DK), bf16)], start_grad, maps)
    end_grads = exchange(end_grads)
    dz, dz_first, filter_grad, scal_grad = kernel_call(
        back_kernel,
        [
            ((TOK, PRE), f32),
            ((HALO, PRE), bf16),
            ((8, PRE), f32),
            ((TOK, TOK), f32),
        ],
        mixed_pre,
        halo,
        filt,
        bdv,
        z,
        q,
        k,
        inverse,
        c_all,
        u_v,
        u_k,
        mixed_grad,
        states,
        end_grads,
        scratch=[pltpu.VMEM((TOK + HALO, PRE), f32)],
    )
    (pre_low,) = kernel_call(
        conv_back_kernel,
        [((TOK, PRE), bf16)],
        dz,
        shift(dz_first, -1),
        filt,
        scratch=[pltpu.VMEM((TOK + HALO, PRE), f32)],
    )
    beta_low = (scal_grad[:, :HEADS] * beta_rows * (1.0 - beta_rows)).astype(bf16)
    decay_grad = scal_grad[:, HEADS : 2 * HEADS]
    decay_pre_grad = decay_grad * decay_rate * jax.nn.sigmoid(decay_at)
    decay_low = decay_pre_grad.astype(bf16)
    log_grad = jnp.sum(decay_grad * decays, axis=0)
    bias_grad = jnp.sum(decay_pre_grad, axis=0)

    part = (
        dot_t(pre_low[:, :QK], w_query)
        + dot_t(pre_low[:, QK : 2 * QK], w_key)
        + dot_t(pre_low[:, 2 * QK :], w_value)
        + dot_t(gate_pre_low, w_outgate)
        + dot_t(beta_low, w_beta)
        + dot_t(decay_low, w_decay)
    ).astype(bf16)
    part = jnp.concatenate(
        [part, jnp.pad(gain_grad.astype(bf16), ((0, 15), (0, width - DV)))], axis=0
    )
    total = part.astype(f32) + swap_tensor(part).astype(f32)
    normed_grad = total[:TOK]
    gain_total = total[TOK, :DV]
    grad_norm_mix = jnp.sum(normed_grad * unit_mix, axis=0)
    grad_inputs = (middle_grad + norm_back(normed_grad, gain_mix, root_mix, unit_mix)).astype(bf16)

    late_sent = weight_grads(
        [(normed_low, jnp.where(first, pre_low[:, 2 * QK :], pre_low[:, : 2 * QK]))]
    )
    late = weight_grads(
        [(normed_low, jnp.where(first, pre_low[:, : 2 * QK], pre_low[:, 2 * QK :]))],
        [swap_core(late_sent)],
    )
    head_grads = jnp.concatenate([log_grad, bias_grad])
    head_high = head_grads.astype(bf16).astype(f32)
    head_parts = jnp.concatenate([head_high, head_grads - head_high])
    taps = filter_grad[0:4].T
    smalls = jnp.concatenate(
        [
            grad_norm_mix.reshape(SEQ, -1),
            grad_norm_ffn.reshape(SEQ, -1),
            gain_total.reshape(SEQ, -1),
            lax.dot_general(
                normed_low, beta_low, (((0,), (0,)), ((), ())), preferred_element_type=f32
            ).reshape(SEQ, -1),
            lax.dot_general(
                normed_low, decay_low, (((0,), (0,)), ((), ())), preferred_element_type=f32
            ).reshape(SEQ, -1),
            taps[:QK].reshape(SEQ, -1),
            taps[QK : 2 * QK].reshape(SEQ, -1),
            taps[2 * QK :].reshape(SEQ, -1),
            jnp.broadcast_to(head_parts, (SEQ, 4 * HEADS)),
        ],
        axis=1,
    ).astype(bf16)
    small_count = smalls.shape[1]
    smalls = jnp.pad(smalls, ((0, 0), (0, 2048 - small_count))).reshape(SEQ, 16, 128)
    late_rows = late.shape[1] + 16
    blocks = placed_call(
        spread_body,
        [(4, SPLIT, 128)] * 4 + [(4, late_rows - SPLIT, 128)] * 4,
        place,
        late,
        smalls,
        swap_core(smalls),
    )
    moved = [blocks[0]] + [lax.ppermute(blocks[s], "seq", along_x(s)) for s in range(1, 4)]
    moved += [blocks[4]] + [lax.ppermute(blocks[4 + s], "seq", along_z(s)) for s in range(1, 4)]
    blocks = placed_call(
        spread_again_body,
        [(SPLIT, 128)] * 4 + [(late_rows - SPLIT, 128)] * 4,
        place,
        *moved,
    )
    moved = [blocks[0]] + [lax.ppermute(blocks[s], "seq", along_z(s)) for s in range(1, 4)]
    moved += [blocks[4]] + [lax.ppermute(blocks[4 + s], "seq", along_x(s)) for s in range(1, 4)]
    (late,) = placed_call(gather_body, [(late_rows, 128)], place, *moved)

    early_first, early_second = over_dp(early.reshape(-1, 128))
    late_first, late_second = over_dp(late)
    gate_rows = 64 * (w_gate.shape[1] // 128)
    down_rows = 96 * (half // 128)
    grad_gate = tiles_to_rows(early_first[:gate_rows], 64, 64)
    grad_up = tiles_to_rows(early_second[:gate_rows], 64, 64)
    grad_down = jnp.concatenate(
        [
            tiles_to_rows(part_rows[gate_rows : gate_rows + down_rows], 88, 96)
            for part_rows in (early_first, early_second)
        ],
        axis=1,
    )
    grad_outgate = tiles_to_rows(early_first[gate_rows + down_rows :], 64, 64)
    grad_wout = tiles_to_rows(early_second[gate_rows + down_rows :], 64, 64)
    late_count = late_rows - 16
    grad_qk = tiles_to_rows(late_first[:late_count], 64, 64)
    grad_value = tiles_to_rows(late_second[:late_count], 64, 64)
    flat = late_first[late_count:].reshape(-1)

    sizes = [64, 64, 16, 64 * HEADS, 64 * HEADS, 32 * 4, 32 * 4, 64 * 4, 4 * HEADS]
    shares = []
    start = 0
    for size in sizes:
        shares.append(flat[start : start + size])
        start += size
    head_total = shares[8].astype(f32)
    head_total = (head_total[: 2 * HEADS] + head_total[2 * HEADS :]).astype(bf16)
    return (
        output.reshape(inputs.shape),
        grad_inputs.reshape(inputs.shape),
        shares[0],
        grad_qk[:, :QK],
        grad_qk[:, QK:],
        grad_value,
        grad_outgate,
        shares[3].reshape(64, HEADS),
        shares[4].reshape(64, HEADS),
        head_total[:HEADS],
        head_total[HEADS:],
        shares[5].reshape(32, 4),
        shares[6].reshape(32, 4),
        shares[7].reshape(64, 4),
        shares[2],
        grad_wout,
        shares[1],
        grad_gate,
        grad_up,
        grad_down,
    )


def solution(mesh):
    return jax.shard_map(
        per_device,
        mesh=mesh,
        in_specs=(
            P("dp", "seq", None),
            P("dp", "seq", None),
            P(),
            P(None, "tensor"),
            P(None, "tensor"),
            P(None, "tensor"),
            P(None, "tensor"),
            P(None, "tensor"),
            P(None, "tensor"),
            P("tensor"),
            P("tensor"),
            P("tensor", None),
            P("tensor", None),
            P("tensor", None),
            P(),
            P("tensor", None),
            P(),
            P(None, "tensor"),
            P(None, "tensor"),
            P("tensor", None),
        ),
        out_specs=(
            P("dp", "seq", None),
            P("dp", "seq", None),
            P("seq"),
            P("seq", "tensor"),
            P("seq", "tensor"),
            P("seq", "tensor"),
            P("seq", "tensor"),
            P("seq", "tensor"),
            P("seq", "tensor"),
            P("tensor"),
            P("tensor"),
            P(("tensor", "seq"), None),
            P(("tensor", "seq"), None),
            P(("tensor", "seq"), None),
            P("seq"),
            P(("tensor", "seq"), None),
            P("seq"),
            P("seq", "tensor"),
            P("seq", "tensor"),
            P(("tensor", "seq"), None),
        ),
        check_vma=False,
    )
```

```python
import functools
import math

import jax
import jax.numpy as jnp
from jax import lax
from jax.experimental import pallas as pl
from jax.experimental.pallas import tpu as pltpu
from jax.sharding import PartitionSpec as P

f32 = jnp.float32
bf16 = jnp.bfloat16
epsilon = 1e-05
smallest = 1e-06
TOK = 128
HEADS = 4
DK = 128
DV = 256
QK = HEADS * DK
VW = HEADS * DV
PRE = 2 * QK + VW
SEQ = 16
HALO = 16
MIB = 1024 * 1024


def kernel_call(body, outs, *args, scratch=(), spare=4 * MIB, flops=0, far=(), far_outs=(), main=()):
    out_shape = [
        pltpu.HBM(shape, kind) if n in far_outs or n in main else jax.ShapeDtypeStruct(shape, kind)
        for n, (shape, kind) in enumerate(outs)
    ]
    moved = sum(a.size * a.dtype.itemsize for a in args)
    for shape, kind in outs:
        moved += math.prod(shape) * jnp.dtype(kind).itemsize
    limit = moved + spare
    return pl.pallas_call(
        body,
        out_shape=out_shape,
        in_specs=[
            pl.BlockSpec(memory_space=pltpu.HBM if n in far else pltpu.VMEM)
            for n in range(len(args))
        ],
        out_specs=[
            pl.BlockSpec(memory_space=pltpu.HBM if n in far_outs else pltpu.VMEM)
            for n in range(len(outs))
        ],
        scratch_shapes=list(scratch),
        compiler_params=pltpu.CompilerParams(vmem_limit_bytes=limit),
        cost_estimate=pl.CostEstimate(flops=flops, bytes_accessed=moved, transcendentals=0),
    )(*args)


def mm(a, b):
    return jnp.dot(a.astype(bf16), b.astype(bf16), preferred_element_type=f32)


def mt(a, b):
    return lax.dot_general(
        a.astype(bf16), b.astype(bf16), (((1,), (1,)), ((), ())), preferred_element_type=f32
    )


def tm(a, b):
    return lax.dot_general(
        a.astype(bf16), b.astype(bf16), (((0,), (0,)), ((), ())), preferred_element_type=f32
    )


def halves(a):
    high = a.astype(bf16)
    return high, (a - high.astype(f32)).astype(bf16)


def mm3(a, b):
    ah, al = halves(a)
    bh, bl = halves(b)
    return mm(jnp.concatenate([ah, al, ah], axis=1), jnp.concatenate([bh, bh, bl], axis=0))


def mm2(a, b):
    ah, al = halves(a)
    return mm(jnp.concatenate([ah, al], axis=1), jnp.concatenate([b, b], axis=0))


def thirds(a):
    high = a.astype(bf16)
    rest = a - high.astype(f32)
    mid = rest.astype(bf16)
    return high, mid, (rest - mid.astype(f32)).astype(bf16)


def masks():
    rows = lax.broadcasted_iota(jnp.int32, (TOK, TOK), 0)
    cols = lax.broadcasted_iota(jnp.int32, (TOK, TOK), 1)
    return rows, cols


def sigmoid(v):
    return 1.0 / (1.0 + jnp.exp(-v))


def fading_of(c_col, c_row, inclusive):
    return jnp.where(inclusive, jnp.exp(jnp.where(inclusive, c_col - c_row, 0.0)), 0.0)


AT_Q = PRE
AT_K = PRE + QK
AT_U = PRE + 2 * QK
KEPT_LOW = ((TOK + HALO, PRE + 3 * QK), bf16)
AT_X = VW
AT_C = VW + QK
AT_B = AT_C + TOK
AT_S = AT_B + TOK
KEPT = ((TOK + 8, PRE), f32)


def front_kernel(
    pre, halo, filt, bdv, slopes, low_hbm, kept_hbm, out_o, send_o, ext, low_o, kept_o, sems
):
    low_o[0:HALO, 0:PRE] = halo[...]
    low_o[HALO:, 0:PRE] = pre[...]
    low_o[TOK:, PRE:] = jnp.zeros((HALO, 3 * QK), bf16)
    ext[0:HALO] = halo[...].astype(f32)
    ext[HALO:] = pre[...].astype(f32)
    kept_o[TOK:, :] = filt[...]
    kept_o[0:TOK, AT_B : AT_B + TOK] = bdv[...]
    kept_o[0:TOK, AT_S : AT_S + TOK] = slopes[...]
    kept_o[0:TOK, AT_S + TOK :] = jnp.zeros((TOK, PRE - AT_S - TOK), f32)

    def activated(at, width):
        z = ext[pl.ds(HALO - 3, TOK), at : at + width] * filt[0:1, at : at + width]
        for j in range(1, 4):
            z = z + ext[pl.ds(HALO - 3 + j, TOK), at : at + width] * filt[j : j + 1, at : at + width]
        return z * sigmoid(z)

    rows, cols = masks()
    inclusive = rows >= cols
    strict = rows > cols
    lower = jnp.where(inclusive, 1.0, 0.0).astype(bf16)
    eye = jnp.where(rows == cols, 1.0, 0.0)
    scal = bdv[...]
    c_all = mm(
        jnp.concatenate([lower, lower, lower], axis=1), jnp.concatenate(thirds(scal), axis=0)
    )
    kept_o[0:TOK, AT_C : AT_C + TOK] = c_all
    c_t = c_all.T
    b_t = scal.T
    heads = range(HEADS)
    qs, ks, vs, lows, invs, fadings = [], [], [], [], [], []
    for h in heads:
        a_q = activated(h * DK, DK)
        a_k = activated(QK + h * DK, DK)
        q = (
            a_q
            * lax.rsqrt(jnp.sum(a_q * a_q, axis=1, keepdims=True) + smallest)
            * DK ** (-0.5)
        ).astype(bf16)
        k = (a_k * lax.rsqrt(jnp.sum(a_k * a_k, axis=1, keepdims=True) + smallest)).astype(bf16)
        low_o[0:TOK, AT_Q + h * DK : AT_Q + (h + 1) * DK] = q
        low_o[0:TOK, AT_K + h * DK : AT_K + (h + 1) * DK] = k
        qs.append(q)
        ks.append(k)
        fading = fading_of(
            c_all[:, HEADS + h : HEADS + h + 1], c_t[HEADS + h : HEADS + h + 1, :], inclusive
        )
        fadings.append(fading)
        lows.append(jnp.where(strict, fading * b_t[h : h + 1, :] * mt(k, k), 0.0))
    pairs = (rows // 2 == cols // 2) & strict
    invs = [eye - jnp.where(pairs, low, 0.0) for low in lows]
    size = 2
    while size < TOK:
        part = (
            (rows // (2 * size) == cols // (2 * size))
            & (rows // size % 2 == 1)
            & (cols // size % 2 == 0)
        )
        steps = [mm3(jnp.where(part, lows[h], 0.0), invs[h]) for h in heads]
        invs = [invs[h] - mm3(invs[h], steps[h]) for h in heads]
        size *= 2
    vs = [activated(2 * QK + h * DV, DV).astype(bf16) for h in heads]
    u_vs = [mm2(invs[h], vs[h]) for h in heads]
    u_ks = [mm2(invs[h] * jnp.exp(c_t[HEADS + h : HEADS + h + 1, :]), ks[h]) for h in heads]
    for h in heads:
        u_v, u_k, q, k = u_vs[h], u_ks[h], qs[h], ks[h]
        c_col = c_all[:, HEADS + h : HEADS + h + 1]
        b_col = scal[:, h : h + 1]
        kept_o[0:TOK, AT_X + h * TOK : AT_X + (h + 1) * TOK] = invs[h]
        kept_o[0:TOK, h * DV : (h + 1) * DV] = u_v
        low_o[0:TOK, AT_U + h * DK : AT_U + (h + 1) * DK] = u_k.astype(bf16)
        scores = fadings[h] * mt(q, k) * b_t[h : h + 1, :]
        out_o[:, h * DV : (h + 1) * DV] = mm(scores, u_v)
        out_o[:, VW + h * DK : VW + (h + 1) * DK] = (
            jnp.exp(c_col) * q.astype(f32) - mm(scores, u_k)
        )
        c_last = c_all[TOK - 1 : TOK, HEADS + h : HEADS + h + 1]
        b_k = b_col * jnp.exp(c_last - c_col) * k.astype(f32)
        turned = (eye * jnp.exp(c_last) - tm(u_k, b_k)).astype(bf16)
        offset = tm(u_v, b_k).astype(bf16)
        for g in range(4):
            send_o[h * 4 + g, 0:DK] = turned
            send_o[h * 4 + g, DK : DK + 64] = offset[64 * g : 64 * g + 64]
    copies = [
        pltpu.make_async_copy(low_o, low_hbm, sems.at[0]),
        pltpu.make_async_copy(kept_o, kept_hbm, sems.at[1]),
    ]
    for copy in copies:
        copy.start()
    for copy in copies:
        copy.wait()


def scan_kernel(maps, out):
    state = jnp.zeros((64, DK), f32)
    for d in range(SEQ):
        out[d] = state.astype(bf16)
        if d < SEQ - 1:
            turned = maps[d, 0:DK]
            state = mm(
                jnp.concatenate(halves(state), axis=1), jnp.concatenate([turned, turned], axis=0)
            ) + maps[d, DK : DK + 64].astype(f32)


def scan_back_kernel(grads, maps, out):
    state = jnp.zeros((64, DK), f32)
    for d in range(SEQ - 1, -1, -1):
        out[d] = state.astype(bf16)
        if d > 0:
            turned = maps[d, 0:DK]
            state = mt(
                jnp.concatenate(halves(state), axis=1), jnp.concatenate([turned, turned], axis=1)
            ) + grads[d].astype(f32)


def mixed_kernel(out_hbm, st, gate_hbm, gain, mixed_o, gated_o, out, gate_pre, sems):
    finish_copies(fetch([(out_hbm, out), (gate_hbm, gate_pre)], sems))
    for h in range(HEADS):
        at = slice(h * DV, (h + 1) * DV)
        state = st[4 * h : 4 * h + 4].reshape(DV, DK)
        mixed = out[:, at] + mt(out[:, VW + h * DK : VW + (h + 1) * DK], state)
        mixed_o[:, at] = mixed
        normed = mixed * lax.rsqrt(jnp.mean(mixed * mixed, axis=1, keepdims=True) + epsilon)
        gate = gate_pre[:, at]
        gated_o[:, at] = (normed * gain[...] * (gate * sigmoid(gate))).astype(bf16)


def mixed_back_kernel(gated_grad, mixed_in, gate_pre, gain, out, do_o, gp_o, gain_o, sg_o):
    gain_total = jnp.zeros((1, DV), f32)
    for h in range(HEADS):
        at = slice(h * DV, (h + 1) * DV)
        mixed = mixed_in[:, at]
        root = lax.rsqrt(jnp.mean(mixed * mixed, axis=1, keepdims=True) + epsilon)
        m = mixed * root
        gate = gate_pre[:, at]
        sig = sigmoid(gate)
        grad = gated_grad[:, at]
        gm = grad * m
        silu = gate * sig
        gain_total = gain_total + jnp.sum(gm * silu, axis=0, keepdims=True)
        gp_o[:, at] = (gm * gain[...] * (sig * (1.0 + gate * (1.0 - sig)))).astype(bf16)
        e = grad * gain[...] * silu
        d_out = (root * (e - m * jnp.mean(e * m, axis=1, keepdims=True))).astype(bf16)
        do_o[:, at] = d_out
        sg = tm(d_out, out[:, VW + h * DK : VW + (h + 1) * DK])
        sg_o[4 * h : 4 * h + 4] = sg.astype(bf16).reshape(4, 64, DK)
    gain_o[...] = gain_total


def back_kernel(
    low_hbm, kept_hbm, do_hbm, st_hbm, gt_i, dz_o, dzh_o, fg_o, low_o, head_o,
    ext, low_i, kept_i, do_i, st_i, sems,
):
    copies = [
        pltpu.make_async_copy(source, target, sems.at[n])
        for n, (source, target) in enumerate(
            ((low_hbm, low_i), (kept_hbm, kept_i), (do_hbm, do_i), (st_hbm, st_i))
        )
    ]
    for copy in copies:
        copy.start()
    for copy in copies:
        copy.wait()
    ext[...] = low_i[:, 0:PRE].astype(f32)
    filt = kept_i[TOK:, :]
    rows, cols = masks()
    inclusive = rows >= cols
    strict = rows > cols
    scal = kept_i[0:TOK, AT_B : AT_B + TOK]
    c_all = kept_i[0:TOK, AT_C : AT_C + TOK]
    c_t = c_all.T
    b_t = scal.T

    def before_silu(at, width):
        z = ext[pl.ds(HALO - 3, TOK), at : at + width] * filt[0:1, at : at + width]
        for j in range(1, 4):
            z = z + ext[pl.ds(HALO - 3 + j, TOK), at : at + width] * filt[j : j + 1, at : at + width]
        return z

    def finish(grad, z, sig, at, width):
        dz = grad * (sig * (1.0 + z * (1.0 - sig)))
        dz_o[:, at : at + width] = dz
        dzh_o[:, at : at + width] = dz[0:HALO].astype(bf16)
        for j in range(4):
            fg_o[j : j + 1, at : at + width] = jnp.sum(
                dz * ext[pl.ds(HALO - 3 + j, TOK), at : at + width], axis=0, keepdims=True
            )

    fg_o[4:8, :] = jnp.zeros((4, PRE), f32)
    lane = lax.broadcasted_iota(jnp.int32, (TOK, TOK), 1)
    cols_acc = jnp.zeros((TOK, TOK), f32)
    sub = lax.broadcasted_iota(jnp.int32, (TOK, TOK), 0)
    rows_acc = jnp.zeros((TOK, TOK), f32)
    heads = range(HEADS)
    at_v = [slice(h * DV, (h + 1) * DV) for h in heads]
    q = [low_i[0:TOK, AT_Q + h * DK : AT_Q + (h + 1) * DK] for h in heads]
    k = [low_i[0:TOK, AT_K + h * DK : AT_K + (h + 1) * DK] for h in heads]
    st = [st_i[4 * h : 4 * h + 4].reshape(DV, DK) for h in heads]
    gt = [gt_i[4 * h : 4 * h + 4].reshape(DV, DK) for h in heads]
    c_col = [c_all[:, HEADS + h : HEADS + h + 1] for h in heads]
    c_row = [c_t[HEADS + h : HEADS + h + 1, :] for h in heads]
    c_last = [c_all[TOK - 1 : TOK, HEADS + h : HEADS + h + 1] for h in heads]
    b_col = [scal[:, h : h + 1] for h in heads]
    b_row = [b_t[h : h + 1, :] for h in heads]
    fading = [fading_of(c_col[h], c_row[h], inclusive) for h in heads]
    growth = [jnp.exp(c_col[h]) for h in heads]
    remains = [jnp.exp(c_last[h] - c_col[h]) for h in heads]
    scores = [fading[h] * mt(q[h], k[h]) for h in heads]
    low_one = [jnp.where(strict, fading[h] * mt(k[h], k[h]), 0.0) for h in heads]
    u = [
        kept_i[0:TOK, at_v[h]]
        - mt(low_i[0:TOK, AT_U + h * DK : AT_U + (h + 1) * DK], st[h])
        for h in heads
    ]
    w = [(b_col[h] * u[h]).astype(bf16) for h in heads]
    k_rem = [remains[h] * k[h].astype(f32) for h in heads]
    d_w = [tm(scores[h], do_i[:, at_v[h]]) + mt(k_rem[h], gt[h]) for h in heads]
    d_beta = [jnp.sum(u[h] * d_w[h], axis=1, keepdims=True) for h in heads]
    d_r = [
        tm(kept_i[0:TOK, AT_X + h * TOK : AT_X + (h + 1) * TOK], b_col[h] * d_w[h]) for h in heads
    ]
    d_rl = [d_r[h].astype(bf16) for h in heads]
    d_low = [jnp.where(strict, -mt(d_rl[h], u[h]), 0.0) for h in heads]
    d_a = [jnp.where(inclusive, mt(do_i[:, at_v[h]], w[h]), 0.0) for h in heads]
    d_qk = [d_a[h] * fading[h] for h in heads]
    e_beta = [d_low[h] * low_one[h] for h in heads]
    e_sum = [d_a[h] * scores[h] + e_beta[h] * b_row[h] for h in heads]
    d_kk = [d_low[h] * fading[h] * b_row[h] for h in heads]
    d_os = [mm(do_i[:, at_v[h]], st[h]) for h in heads]
    d_rs = [mm(d_rl[h], st[h]) for h in heads]
    w_g = [mm(w[h], gt[h]) for h in heads]
    dq = [mm(d_qk[h], k[h]) + growth[h] * d_os[h] for h in heads]
    dk = [
        tm(d_qk[h], q[h])
        + mm(d_kk[h], k[h])
        + tm(d_kk[h], k[h])
        - growth[h] * d_rs[h]
        + remains[h] * w_g[h]
        for h in heads
    ]
    for h in heads:
        rem_sum = jnp.sum(k_rem[h] * w_g[h], axis=1, keepdims=True)
        d_c = (
            jnp.sum(e_sum[h], axis=1, keepdims=True)
            + growth[h]
            * jnp.sum(
                q[h].astype(f32) * d_os[h] - k[h].astype(f32) * d_rs[h], axis=1, keepdims=True
            )
            - rem_sum
        )
        last = jnp.sum(rem_sum, axis=0, keepdims=True) + jnp.exp(c_last[h]) * jnp.sum(
            jnp.sum(st[h].astype(f32) * gt[h].astype(f32), axis=1, keepdims=True),
            axis=0,
            keepdims=True,
        )
        d_c = d_c + jnp.where(sub[:, 0:1] == TOK - 1, last, 0.0)
        cols_acc = cols_acc + jnp.where(lane == h, d_beta[h], 0.0)
        cols_acc = cols_acc + jnp.where(lane == HEADS + h, d_c, 0.0)
        rows_acc = rows_acc + jnp.where(sub == h, jnp.sum(e_beta[h], axis=0, keepdims=True), 0.0)
        rows_acc = rows_acc - jnp.where(
            sub == HEADS + h, jnp.sum(e_sum[h], axis=0, keepdims=True), 0.0
        )
    for h in heads:
        for grad, base, scale in ((dq[h], 0, DK ** (-0.5)), (dk[h], QK, 1.0)):
            at = base + h * DK
            z = before_silu(at, DK)
            sig = sigmoid(z)
            act = z * sig
            root = lax.rsqrt(jnp.sum(act * act, axis=1, keepdims=True) + smallest)
            unit = act * root
            grad = grad * scale
            d_act = root * (grad - unit * jnp.sum(unit * grad, axis=1, keepdims=True))
            finish(d_act, z, sig, at, DK)
        at = 2 * QK + h * DV
        z = before_silu(at, DV)
        finish(d_r[h], z, sigmoid(z), at, DV)
    total = cols_acc + rows_acc.T
    upper = jnp.where(rows <= cols, 1.0, 0.0).astype(bf16)
    summed = mm(
        jnp.concatenate([upper, upper, upper], axis=1), jnp.concatenate(thirds(total), axis=0)
    )
    grads = jnp.where(lane < HEADS, total, summed)
    sloped = grads * kept_i[0:TOK, AT_S : AT_S + TOK]
    low_o[...] = sloped.astype(bf16)
    head_o[0:1, :] = jnp.sum(grads * scal, axis=0, keepdims=True)
    head_o[1:2, :] = jnp.sum(sloped, axis=0, keepdims=True)
    head_o[2:8, :] = jnp.zeros((6, TOK), f32)


def conv_back_kernel(dz, after, filt, pre_o, ext):
    ext[0:TOK] = dz[...]
    ext[TOK:] = after[...].astype(f32)
    for at in range(0, PRE, 256):
        total = ext[pl.ds(3, TOK), at : at + 256] * filt[0:1, at : at + 256]
        for j in range(1, 4):
            total = total + ext[pl.ds(3 - j, TOK), at : at + 256] * filt[j : j + 1, at : at + 256]
        pre_o[:, at : at + 256] = total.astype(bf16)


def input_grad_kernel(part, part_in, middle_grad, inputs, gain_mix, grad_o):
    grad = part[...].astype(f32) + part_in[...].astype(f32)
    values = inputs[...].astype(f32)
    root = lax.rsqrt(jnp.mean(values * values, axis=1, keepdims=True) + epsilon)
    unit = values * root
    e = grad * gain_mix[...]
    grad_o[...] = (
        middle_grad[...] + root * (e - unit * jnp.mean(e * unit, axis=1, keepdims=True))
    ).astype(bf16)


def smalls_kernel(part, inputs, gain, ffn_gain_grad, normed, logits, taps, heads, small_o):
    values = inputs[...].astype(f32)
    root = lax.rsqrt(jnp.mean(values * values, axis=1, keepdims=True) + epsilon)
    mix_grad = jnp.sum(part[...].astype(f32) * (values * root), axis=0, keepdims=True)
    gain_grad = gain[...]
    logit_grads = tm(logits[...], normed[...])[0:8]
    log_grad = heads[0:1, HEADS : 2 * HEADS]
    bias_grad = heads[1:2, HEADS : 2 * HEADS]
    head = jnp.concatenate([log_grad, bias_grad], axis=1)
    high = head.astype(bf16).astype(f32)
    head = jnp.concatenate([high, head - high, jnp.zeros((1, 64 - 4 * HEADS), f32)], axis=1)
    ffn = ffn_gain_grad[...]
    tap = taps[0:4, :]
    for j in range(SEQ):
        wide = slice(64 * j, 64 * j + 64)
        small_o[j] = jnp.concatenate(
            [
                jnp.concatenate([mix_grad[:, wide], ffn[:, wide]], axis=1),
                jnp.concatenate(
                    [gain_grad[:, 16 * j : 16 * j + 16], jnp.zeros((1, 48), f32), head], axis=1
                ),
                jnp.zeros((2, 128), f32),
                jnp.concatenate([logit_grads[0:4, wide], logit_grads[4:8, wide]], axis=1),
                jnp.concatenate(
                    [
                        tap[:, 2 * QK + 64 * j : 2 * QK + 64 * j + 64],
                        tap[:, 32 * j : 32 * j + 32],
                        tap[:, QK + 32 * j : QK + 32 * j + 32],
                    ],
                    axis=1,
                ),
                jnp.zeros((4, 128), f32),
            ],
            axis=0,
        ).astype(bf16)


def padded_rows(left):
    return -(-(left.shape[1] // SEQ) // 16) * 16


def pieces_rows(pieces):
    return sum(padded_rows(left) * (right.shape[1] // 128) for left, right in pieces)


def weight_body(count, added, refs):
    ins = refs[: 2 * count]
    adds = refs[2 * count : 2 * count + added]
    out = refs[2 * count + added]
    turned = refs[2 * count + added + 1]
    offset = 0
    part = 0
    done = 0
    for at in range(count):
        left, right = ins[2 * at], ins[2 * at + 1]
        width = left.shape[1]
        rows = width // SEQ
        padded = padded_rows(left)
        turned[0:width] = left[...].T

        def tiles(n, count, right=right, width=width, rows=rows, padded=padded, offset=offset,
                  part=part, done=done):
            wide = jnp.dot(
                turned[0:width],
                right[:, pl.ds(pl.multiple_of(n * 128, 128), 128 * count)],
                preferred_element_type=f32,
            )
            for m in range(count):
                piece = wide[:, m * 128 : (m + 1) * 128].reshape(SEQ, rows, 128)
                if padded > rows:
                    piece = jnp.concatenate(
                        [piece, jnp.zeros((SEQ, padded - rows, 128), f32)], axis=1
                    )
                if part < added:
                    where = pl.ds(pl.multiple_of(offset - done + (n + m) * padded, 16), padded)
                    piece = piece + adds[part][:, where].astype(f32)
                where = pl.ds(pl.multiple_of(offset + (n + m) * padded, 16), padded)
                out[:, where] = piece.astype(bf16)

        def pair(n, carry, tiles=tiles):
            tiles(2 * n, 2)
            return carry

        count_here = right.shape[1] // 128
        lax.fori_loop(0, count_here // 2, pair, 0)
        if count_here % 2:
            tiles(count_here - 1, 1)
        offset += padded * (right.shape[1] // 128)
        if part < added and offset - done == adds[part].shape[1]:
            done = offset
            part += 1


def weight_grads(pieces, adds=()):
    total = pieces_rows(pieces)
    args = [operand for pair in pieces for operand in pair] + list(adds)

    def body(*refs):
        weight_body(len(pieces), len(adds), refs)

    return kernel_call(
        body,
        [((SEQ, total, 128), bf16)],
        *args,
        scratch=[pltpu.VMEM((1408, TOK), bf16)],
        spare=6 * MIB,
        flops=2 * 128 * 128 * SEQ * total,
        main=(0,),
    )[0]


def fetch(pairs, sems, first=0):
    copies = [
        pltpu.make_async_copy(source, target, sems.at[first + n])
        for n, (source, target) in enumerate(pairs)
    ]
    for copy in copies:
        copy.start()
    return copies


def finish_copies(copies):
    for copy in copies:
        copy.wait()


def late_body(place, normed, pre_kept, late_in, smalls, *refs):
    outs = refs[0:8]
    turned, kept, late_add, sems = refs[8:]
    rows = kept.shape[2] // 2
    fetched = fetch([(late_in, late_add)], sems)
    sent = []
    for s in range(4):
        x_to = lax.rem(place[1] + s, 4)
        sent += fetch([(smalls.at[:, x_to], outs[s].at[:, pl.ds(rows, 16)])], sems, 1 + s)
    turned[...] = normed[...].T
    finish_copies(fetched)
    for n in range(pre_kept.shape[1] // 256):
        wide = jnp.dot(
            turned[...], pre_kept[:, n * 256 : (n + 1) * 256], preferred_element_type=f32
        )
        for m in range(2):
            where = slice((2 * n + m) * 64, (2 * n + m + 1) * 64)
            piece = wide[:, m * 128 : (m + 1) * 128].reshape(SEQ, 64, 128)
            piece = piece + late_add[:, where].astype(f32)
            kept[:, :, where] = piece.astype(bf16).reshape(4, 4, 64, 128)
        if 2 * (n + 1) * 64 == rows:
            for s in range(4):
                x_to = lax.rem(place[1] + s, 4)
                sent += fetch(
                    [(kept.at[:, x_to, pl.ds(0, rows)], outs[s].at[:, pl.ds(0, rows)])], sems, 5 + s
                )
    for s in range(4):
        z_to = lax.rem(place[0] + s, 4)
        sent += fetch([(kept.at[z_to, :, pl.ds(rows, rows)], outs[4 + s])], sems, 9 + s)
    finish_copies(sent)


def in_order(terms, own):
    total = None
    for source in range(4):
        which = lax.rem(own + 4 - source, 4)
        term = jnp.zeros(terms[0].shape, f32)
        for n in range(4):
            term = jnp.where(which == n, terms[n].astype(f32), term)
        total = term if total is None else total + term
    return total


def plain_sum(terms):
    total = terms[0].astype(f32)
    for term in terms[1:]:
        total = total + term.astype(f32)
    return total


def sum_spread_body(place, *refs):
    outs, parts, sems = refs[8:16], refs[16:24], refs[24]
    finish_copies(fetch(zip(refs[0:8], parts), sems))
    first, second = parts[0:4], parts[4:8]
    rows = first[0].shape[1]
    for s in range(4):
        z_to = lax.rem(place[0] + s, 4)
        x_to = lax.rem(place[1] + s, 4)
        outs[s][...] = plain_sum([part[z_to] for part in first]).astype(bf16)
        outs[s][rows - 16 :] = in_order(
            [part[z_to, rows - 16 : rows] for part in first], place[1]
        ).astype(bf16)
        outs[4 + s][...] = plain_sum([part[x_to] for part in second]).astype(bf16)


def sum_body(place, *refs):
    out, parts, sems = refs[8], refs[9:17], refs[17]
    finish_copies(fetch(zip(refs[0:8], parts), sems))
    first, second = parts[0:4], parts[4:8]
    rows = first[0].shape[0]
    out[0:rows] = plain_sum([part[...] for part in first]).astype(bf16)
    out[rows - 16 : rows] = in_order(
        [part[rows - 16 : rows] for part in first], place[0]
    ).astype(bf16)
    out[rows:] = plain_sum([part[...] for part in second]).astype(bf16)


def fill(first, mine, other, out, core, at, rows=64, padded=64, count=None, first_tile=0):
    same = first if core == 0 else jnp.logical_not(first)
    for n in range(out.shape[1] // 128 if count is None else count):
        spot = slice(at + n * padded, at + n * padded + padded)
        block = jnp.where(same, mine[spot].astype(f32), other[spot].astype(f32))
        column = (first_tile + n) * 128
        out[:, column : column + 128] = block.astype(bf16)[0:rows]


def unpack_early_body(place, mine, other, gate_o, up_o, down_o, outgate_o, wout_o):
    put = functools.partial(fill, place[2] == 0, mine, other)
    put(gate_o, 0, 0)
    put(up_o, 1, 0)
    at = gate_o.shape[1] // 128 * 64
    tiles = down_o.shape[1] // 256
    put(down_o, 0, at, 88, 96, tiles)
    put(down_o, 1, at, 88, 96, tiles, tiles)
    at += 96 * tiles
    put(outgate_o, 0, at)
    put(wout_o, 1, at)


def unpack_late_body(
    place, mine, other, over_tensor, over_both, query_o, key_o, value_o, mix_o, ffn_o, gain_o,
    log_o, bias_o, beta_o, decay_o, taps_q_o, taps_k_o, taps_v_o,
):
    put = functools.partial(fill, place[2] == 0, mine, other)
    half = VW // 4
    put(query_o, 0, 0)
    put(key_o, 0, half + 16)
    put(value_o, 1, 0, count=4)
    put(value_o, 1, half + 16, count=4, first_tile=4)
    small = mine[half : half + 16].astype(f32) + other[half : half + 16].astype(f32)
    both = small[0:2] + (over_tensor[0:2].astype(f32) + over_both[0:2].astype(f32))
    mix_o[...] = both[0:1, 0:64].astype(bf16)
    ffn_o[...] = small[0:1, 64:128].astype(bf16)
    gain_o[...] = both[1:2, 0:16].astype(bf16)
    for n, out in enumerate((log_o, bias_o)):
        start = 64 + n * HEADS
        out[...] = (
            small[1:2, start : start + HEADS]
            + small[1:2, start + 2 * HEADS : start + 3 * HEADS]
        ).astype(bf16)
    beta_o[...] = small[4:8, 0:64].astype(bf16)
    decay_o[...] = small[4:8, 64:128].astype(bf16)
    taps_q_o[...] = small[8:12, 64:96].astype(bf16)
    taps_k_o[...] = small[8:12, 96:128].astype(bf16)
    taps_v_o[...] = small[8:12, 0:64].astype(bf16)


def placed_call(body, outs, place, *args, main=False, far=(), far_outs=(), scratch=(), limit=12):
    kind = pltpu.HBM if main else jax.ShapeDtypeStruct
    return pl.pallas_call(
        body,
        out_shape=[kind(shape, bf16) for shape in outs],
        in_specs=[pl.BlockSpec(memory_space=pltpu.SMEM)]
        + [
            pl.BlockSpec(memory_space=pltpu.HBM if n in far else pltpu.VMEM)
            for n in range(len(args))
        ],
        out_specs=[
            pl.BlockSpec(memory_space=pltpu.HBM if n in far_outs else pltpu.VMEM)
            for n in range(len(outs))
        ],
        scratch_shapes=list(scratch),
        compiler_params=pltpu.CompilerParams(vmem_limit_bytes=limit * MIB),
    )(place, *args)


def along_x(steps):
    return [(z * 4 + x, z * 4 + (x + steps) % 4) for z in range(4) for x in range(4)]


def along_z(steps):
    return [(z * 4 + x, (z + steps) % 4 * 4 + x) for z in range(4) for x in range(4)]


def swap_tensor(value):
    return lax.ppermute(value, "tensor", [(0, 1), (1, 0)])


def swap_core(value):
    return lax.ppermute(value, "dp", [(0, 1), (1, 0), (2, 3), (3, 2)])


def swap_both(value):
    pairs = [(t * 4 + d, (1 - t) * 4 + d // 2 * 2 + 1 - d % 2) for t in range(2) for d in range(4)]
    return lax.ppermute(value, ("tensor", "dp"), pairs)


def swap_far(value):
    return lax.ppermute(value, "dp", [(0, 2), (2, 0), (1, 3), (3, 1)])


def shift(value, steps):
    first, last = max(0, -steps), min(SEQ, SEQ - steps)
    return lax.ppermute(value, "seq", [(at, at + steps) for at in range(first, last)])


def exchange(value):
    return lax.all_to_all(value, "seq", 0, 0, tiled=True)


def dot(a, b):
    return jnp.dot(a, b, preferred_element_type=f32)


def dot_t(a, b):
    return lax.dot_general(a, b, (((1,), (1,)), ((), ())), preferred_element_type=f32)


def norm_parts(values):
    root = lax.rsqrt(jnp.mean(values * values, axis=-1, keepdims=True) + epsilon)
    return root, values * root


def norm_back(grad, gain, root, unit):
    e = grad * gain
    return root * (e - unit * jnp.mean(e * unit, axis=-1, keepdims=True))


def per_device(
    inputs,
    cotangent,
    norm_mix,
    w_query,
    w_key,
    w_value,
    w_outgate,
    w_beta,
    w_decay,
    decay_log,
    decay_bias,
    conv_query,
    conv_key,
    conv_value,
    out_gain,
    w_out,
    norm_ffn,
    w_gate,
    w_up,
    w_down,
):
    width = inputs.shape[2]
    first = lax.axis_index("dp") % 2 == 0
    at = lax.axis_index("seq")
    place = jnp.stack([at // 4, at % 4, lax.axis_index("dp") % 2]).astype(jnp.int32)
    residual = inputs.reshape(TOK, width).astype(f32)
    feed_grad = cotangent.reshape(TOK, width)
    gain_mix = norm_mix.astype(f32)
    gain_ffn = norm_ffn.astype(f32)
    gain_head = out_gain.astype(f32).reshape(1, DV)
    filters = jnp.concatenate([conv_query, conv_key, conv_value], axis=0).astype(f32)
    filt = jnp.pad(filters.T, ((0, 4), (0, 0)))

    root_mix, unit_mix = norm_parts(residual)
    normed_low = (unit_mix * gain_mix).astype(bf16)
    mixed_pre = jnp.concatenate(
        [dot(normed_low, w_query), dot(normed_low, w_key), dot(normed_low, w_value)], axis=1
    ).astype(bf16)
    halo = shift(mixed_pre[TOK - HALO :], 1)
    beta_rows = jax.nn.sigmoid(dot(normed_low, w_beta))
    decay_at = dot(normed_low, w_decay) + decay_bias.astype(f32)
    decay_rate = -jnp.exp(decay_log.astype(f32))
    decays = decay_rate * jax.nn.softplus(decay_at)

    def lanes(values, others):
        return jnp.pad(jnp.concatenate([values, others], axis=1), ((0, 0), (0, 120)))

    bdv = lanes(beta_rows, decays)
    slopes = lanes(beta_rows * (1.0 - beta_rows), decay_rate * jax.nn.sigmoid(decay_at))
    gate_pre = dot(normed_low, w_outgate)

    kept_low, kept, out_local, maps = kernel_call(
        front_kernel,
        [KEPT_LOW, KEPT, ((TOK, VW + QK), f32), ((SEQ, DK + 64, DK), bf16)],
        mixed_pre,
        halo,
        filt,
        bdv,
        slopes,
        scratch=[
            pltpu.VMEM((TOK + HALO, PRE), f32),
            pltpu.VMEM(*KEPT_LOW),
            pltpu.VMEM(*KEPT),
            pltpu.SemaphoreType.DMA((2,)),
        ],
        far_outs=(0, 1),
        main=(3,),
    )
    maps = exchange(maps)
    (states,) = kernel_call(scan_kernel, [((SEQ, 64, DK), bf16)], maps, main=(0,))
    states = exchange(states)
    mixed, gated_low = kernel_call(
        mixed_kernel,
        [((TOK, VW), f32), ((TOK, VW), bf16)],
        out_local,
        states,
        gate_pre,
        gain_head,
        scratch=[
            pltpu.VMEM((TOK, VW + QK), f32),
            pltpu.VMEM((TOK, VW), f32),
            pltpu.SemaphoreType.DMA((2,)),
        ],
        far=(0, 2),
    )
    branch = dot(gated_low, w_out).astype(bf16)
    branch_in = swap_tensor(branch)
    hidden_grad = dot_t(feed_grad, w_down)
    middle = residual + (branch.astype(f32) + branch_in.astype(f32))
    root_ffn, unit_ffn = norm_parts(middle)
    two_low = (unit_ffn * gain_ffn).astype(bf16)
    gate_ffn = dot(two_low, w_gate)
    up_ffn = dot(two_low, w_up)
    sig = jax.nn.sigmoid(gate_ffn)
    silu = gate_ffn * sig
    hidden_low = (silu * up_ffn).astype(bf16)
    gate_low = (hidden_grad * up_ffn * (sig * (1.0 + gate_ffn * (1.0 - sig)))).astype(bf16)
    up_low = (hidden_grad * silu).astype(bf16)
    half = width // 2
    ffn_sent = weight_grads(
        [
            (two_low, jnp.where(first, up_low, gate_low)),
            (hidden_low, jnp.where(first, feed_grad[:, half:], feed_grad[:, :half])),
        ]
    )
    ffn_in = swap_core(ffn_sent)
    ffn_sent, gate_next, up_next = lax.optimization_barrier((ffn_sent, gate_low, up_low))
    two_part = (dot_t(gate_next, w_gate) + dot_t(up_next, w_up)).astype(bf16)
    two_in = swap_tensor(two_part)

    two_grad = two_part.astype(f32) + two_in.astype(f32)
    grad_norm_ffn = jnp.sum(two_grad * unit_ffn, axis=0)
    middle_grad = feed_grad.astype(f32) + norm_back(two_grad, gain_ffn, root_ffn, unit_ffn)
    branch_low = middle_grad.astype(bf16)
    gated_grad = dot_t(branch_low, w_out)
    mixed_grad, gate_pre_low, gain_grad, start_grad = kernel_call(
        mixed_back_kernel,
        [((TOK, VW), bf16), ((TOK, VW), bf16), ((1, DV), f32), ((SEQ, 64, DK), bf16)],
        gated_grad,
        mixed,
        gate_pre,
        gain_head,
        out_local,
        main=(3,),
    )
    out_sent = weight_grads(
        [
            (
                jnp.where(first, gated_low, normed_low),
                jnp.where(first, branch_low, gate_pre_low),
            )
        ]
    )
    early = weight_grads(
        [
            (two_low, jnp.where(first, gate_low, up_low)),
            (hidden_low, jnp.where(first, feed_grad[:, :half], feed_grad[:, half:])),
            (
                jnp.where(first, normed_low, gated_low),
                jnp.where(first, gate_pre_low, branch_low),
            ),
        ],
        [ffn_in, swap_core(out_sent)],
    )
    early = lax.optimization_barrier(
        lax.psum_scatter(early, "seq", scatter_dimension=0, tiled=True)
    )
    start_grad = exchange(start_grad)
    (end_grads,) = kernel_call(
        scan_back_kernel, [((SEQ, 64, DK), bf16)], start_grad, maps, main=(0,)
    )
    end_grads = exchange(end_grads)
    end_grads, hidden_last = lax.optimization_barrier((end_grads, hidden_low))
    feed_part = dot(hidden_last, w_down).astype(bf16)
    feed_in = swap_tensor(feed_part)
    output = (middle + (feed_part.astype(f32) + feed_in.astype(f32))).astype(bf16)
    dz, dz_first, filter_grad, logit_low, head_grads = kernel_call(
        back_kernel,
        [
            ((TOK, PRE), f32),
            ((HALO, PRE), bf16),
            ((8, PRE), f32),
            ((TOK, TOK), bf16),
            ((8, TOK), f32),
        ],
        kept_low,
        kept,
        mixed_grad,
        states,
        end_grads,
        scratch=[
            pltpu.VMEM((TOK + HALO, PRE), f32),
            pltpu.VMEM(*KEPT_LOW),
            pltpu.VMEM(*KEPT),
            pltpu.VMEM((TOK, VW), bf16),
            pltpu.VMEM((SEQ, 64, DK), bf16),
            pltpu.SemaphoreType.DMA((4,)),
        ],
        far=(0, 1, 2, 3),
        main=(1,),
    )
    (pre_low,) = kernel_call(
        conv_back_kernel,
        [((TOK, PRE), bf16)],
        dz,
        shift(dz_first, -1),
        filt,
        scratch=[pltpu.VMEM((TOK + HALO, PRE), f32)],
    )
    part = (
        dot_t(pre_low[:, :QK], w_query)
        + dot_t(pre_low[:, QK : 2 * QK], w_key)
        + dot_t(pre_low[:, 2 * QK :], w_value)
        + dot_t(gate_pre_low, w_outgate)
        + dot_t(logit_low[:, :HEADS], w_beta)
        + dot_t(logit_low[:, HEADS : 2 * HEADS], w_decay)
    ).astype(bf16)
    late_sent = weight_grads(
        [(normed_low, jnp.where(first, pre_low[:, 2 * QK :], pre_low[:, : 2 * QK]))]
    )
    late_in = swap_core(late_sent)
    (smalls,) = kernel_call(
        smalls_kernel,
        [((SEQ, 16, 128), bf16)],
        part,
        inputs.reshape(TOK, width),
        gain_grad,
        grad_norm_ffn.reshape(1, width),
        normed_low,
        logit_low,
        filter_grad,
        head_grads,
    )
    half_rows = VW // 4
    small_rows = half_rows + 16
    blocks = placed_call(
        late_body,
        [(4, small_rows, 128)] * 4 + [(4, half_rows, 128)] * 4,
        place,
        normed_low,
        jnp.where(first, pre_low[:, : 2 * QK], pre_low[:, 2 * QK :]),
        late_in,
        smalls.reshape(4, 4, 16, 128),
        main=True,
        far=(2,),
        far_outs=range(8),
        scratch=[
            pltpu.VMEM((width, TOK), bf16),
            pltpu.VMEM((4, 4, 2 * half_rows, 128), bf16),
            pltpu.VMEM((SEQ, 2 * half_rows, 128), bf16),
            pltpu.SemaphoreType.DMA((13,)),
        ],
        limit=16,
    )
    moved = [blocks[0]] + [lax.ppermute(blocks[s], "seq", along_x(s)) for s in range(1, 4)]
    moved += [blocks[4]] + [lax.ppermute(blocks[4 + s], "seq", along_z(s)) for s in range(1, 4)]
    *blocks, part_next = lax.optimization_barrier((*blocks, part))
    part_in = swap_tensor(part_next)
    (grad_inputs,) = kernel_call(
        input_grad_kernel,
        [((TOK, width), bf16)],
        part_next,
        part_in,
        middle_grad,
        inputs.reshape(TOK, width),
        gain_mix.reshape(1, width),
    )
    *moved, grad_inputs, output = lax.optimization_barrier((*moved, grad_inputs, output))
    step_shapes = [(4, small_rows, 128)] * 4 + [(4, half_rows, 128)] * 4
    blocks = placed_call(
        sum_spread_body,
        [(small_rows, 128)] * 4 + [(half_rows, 128)] * 4,
        place,
        *moved,
        main=True,
        far=range(8),
        scratch=[pltpu.VMEM(shape, bf16) for shape in step_shapes]
        + [pltpu.SemaphoreType.DMA((8,))],
        limit=60,
    )
    moved = [blocks[0]] + [lax.ppermute(blocks[s], "seq", along_z(s)) for s in range(1, 4)]
    moved += [blocks[4]] + [lax.ppermute(blocks[4 + s], "seq", along_x(s)) for s in range(1, 4)]
    *_, early = lax.optimization_barrier((*blocks, early.reshape(-1, 128)))
    early_far = swap_far(early)
    *moved, early, early_far = lax.optimization_barrier((*moved, early, early_far))
    (late,) = placed_call(
        sum_body,
        [(small_rows + half_rows, 128)],
        place,
        *moved,
        main=True,
        far=range(8),
        scratch=[pltpu.VMEM(shape[1:], bf16) for shape in step_shapes]
        + [pltpu.SemaphoreType.DMA((8,))],
        limit=60,
    )
    late, early, early_far = lax.optimization_barrier((late, early, early_far))
    late_far = swap_far(late)
    columns = w_gate.shape[1]
    early = (early.astype(f32) + early_far.astype(f32)).astype(bf16)
    grad_gate, grad_up, grad_down, grad_outgate, grad_wout = placed_call(
        unpack_early_body,
        [(64, columns), (64, columns), (88, width), (64, VW), (64, width)],
        place,
        early,
        swap_core(early),
    )
    late_far, grad_gate, grad_up, grad_down, grad_outgate, grad_wout = lax.optimization_barrier(
        (late_far, grad_gate, grad_up, grad_down, grad_outgate, grad_wout)
    )
    late = (late.astype(f32) + late_far.astype(f32)).astype(bf16)
    small = late[half_rows:small_rows]
    shares = placed_call(
        unpack_late_body,
        [
            (64, QK),
            (64, QK),
            (64, VW),
            (1, 64),
            (1, 64),
            (1, 16),
            (1, HEADS),
            (1, HEADS),
            (4, 64),
            (4, 64),
            (4, 32),
            (4, 32),
            (4, 64),
        ],
        place,
        late,
        swap_core(late),
        swap_tensor(small),
        swap_both(small),
    )
    grad_query, grad_key, grad_value = shares[:3]
    mix, ffn, gain, log, bias, beta, decay, taps_q, taps_k, taps_v = shares[3:]
    return (
        output.reshape(inputs.shape),
        grad_inputs.reshape(inputs.shape),
        mix.reshape(-1),
        grad_query,
        grad_key,
        grad_value,
        grad_outgate,
        beta.T,
        decay.T,
        log.reshape(-1),
        bias.reshape(-1),
        taps_q.T,
        taps_k.T,
        taps_v.T,
        gain.reshape(-1),
        grad_wout,
        ffn.reshape(-1),
        grad_gate,
        grad_up,
        grad_down,
    )


def solution(mesh):
    return jax.shard_map(
        per_device,
        mesh=mesh,
        in_specs=(
            P("dp", "seq", None),
            P("dp", "seq", None),
            P(),
            P(None, "tensor"),
            P(None, "tensor"),
            P(None, "tensor"),
            P(None, "tensor"),
            P(None, "tensor"),
            P(None, "tensor"),
            P("tensor"),
            P("tensor"),
            P("tensor", None),
            P("tensor", None),
            P("tensor", None),
            P(),
            P("tensor", None),
            P(),
            P(None, "tensor"),
            P(None, "tensor"),
            P("tensor", None),
        ),
        out_specs=(
            P("dp", "seq", None),
            P("dp", "seq", None),
            P("seq"),
            P("seq", "tensor"),
            P("seq", "tensor"),
            P("seq", "tensor"),
            P("seq", "tensor"),
            P("seq", "tensor"),
            P("seq", "tensor"),
            P("tensor"),
            P("tensor"),
            P(("tensor", "seq"), None),
            P(("tensor", "seq"), None),
            P(("tensor", "seq"), None),
            P("seq"),
            P(("tensor", "seq"), None),
            P("seq"),
            P("seq", "tensor"),
            P("seq", "tensor"),
            P(("tensor", "seq"), None),
        ),
        check_vma=False,
    )
```

```python
import functools
import math

import jax
import jax.numpy as jnp
from jax import lax
from jax.experimental import pallas as pl
from jax.experimental.pallas import tpu as pltpu
from jax.sharding import PartitionSpec as P

f32 = jnp.float32
bf16 = jnp.bfloat16
epsilon = 1e-05
smallest = 1e-06
TOK = 128
HEADS = 4
DK = 128
DV = 256
QK = HEADS * DK
VW = HEADS * DV
PRE = 2 * QK + VW
SEQ = 16
HALO = 16
MIB = 1024 * 1024


def kernel_call(body, outs, *args, scratch=(), spare=4 * MIB, flops=0, far=(), far_outs=(), main=()):
    out_shape = [
        pltpu.HBM(shape, kind) if n in far_outs or n in main else jax.ShapeDtypeStruct(shape, kind)
        for n, (shape, kind) in enumerate(outs)
    ]
    moved = sum(a.size * a.dtype.itemsize for a in args)
    for shape, kind in outs:
        moved += math.prod(shape) * jnp.dtype(kind).itemsize
    limit = moved + spare
    return pl.pallas_call(
        body,
        out_shape=out_shape,
        in_specs=[
            pl.BlockSpec(memory_space=pltpu.HBM if n in far else pltpu.VMEM)
            for n in range(len(args))
        ],
        out_specs=[
            pl.BlockSpec(memory_space=pltpu.HBM if n in far_outs else pltpu.VMEM)
            for n in range(len(outs))
        ],
        scratch_shapes=list(scratch),
        compiler_params=pltpu.CompilerParams(vmem_limit_bytes=limit),
        cost_estimate=pl.CostEstimate(flops=flops, bytes_accessed=moved, transcendentals=0),
    )(*args)


def mm(a, b):
    return jnp.dot(a.astype(bf16), b.astype(bf16), preferred_element_type=f32)


def mt(a, b):
    return lax.dot_general(
        a.astype(bf16), b.astype(bf16), (((1,), (1,)), ((), ())), preferred_element_type=f32
    )


def tm(a, b):
    return lax.dot_general(
        a.astype(bf16), b.astype(bf16), (((0,), (0,)), ((), ())), preferred_element_type=f32
    )


def halves(a):
    high = a.astype(bf16)
    return high, (a - high.astype(f32)).astype(bf16)


def mm3(a, b):
    ah, al = halves(a)
    bh, bl = halves(b)
    return mm(jnp.concatenate([ah, al, ah], axis=1), jnp.concatenate([bh, bh, bl], axis=0))


def mm2(a, b):
    ah, al = halves(a)
    return mm(jnp.concatenate([ah, al], axis=1), jnp.concatenate([b, b], axis=0))


def thirds(a):
    high = a.astype(bf16)
    rest = a - high.astype(f32)
    mid = rest.astype(bf16)
    return high, mid, (rest - mid.astype(f32)).astype(bf16)


def masks():
    rows = lax.broadcasted_iota(jnp.int32, (TOK, TOK), 0)
    cols = lax.broadcasted_iota(jnp.int32, (TOK, TOK), 1)
    return rows, cols


def sigmoid(v):
    return 1.0 / (1.0 + jnp.exp(-v))


def fading_of(c_col, c_row, inclusive):
    return jnp.where(inclusive, jnp.exp(jnp.where(inclusive, c_col - c_row, 0.0)), 0.0)


AT_Q = PRE
AT_K = PRE + QK
AT_U = PRE + 2 * QK
KEPT_LOW = ((TOK + HALO, PRE + 3 * QK), bf16)
AT_X = VW
AT_C = VW + QK
AT_B = AT_C + TOK
AT_S = AT_B + TOK
KEPT = ((TOK + 8, PRE), f32)


def front_kernel(
    pre, halo, filt, bdv, slopes, low_hbm, kept_hbm, out_o, send_o, ext, low_o, kept_o, sems
):
    low_o[0:HALO, 0:PRE] = halo[...]
    low_o[HALO:, 0:PRE] = pre[...]
    low_o[TOK:, PRE:] = jnp.zeros((HALO, 3 * QK), bf16)
    ext[0:HALO] = halo[...].astype(f32)
    ext[HALO:] = pre[...].astype(f32)
    kept_o[TOK:, :] = filt[...]
    kept_o[0:TOK, AT_B : AT_B + TOK] = bdv[...]
    kept_o[0:TOK, AT_S : AT_S + TOK] = slopes[...]
    kept_o[0:TOK, AT_S + TOK :] = jnp.zeros((TOK, PRE - AT_S - TOK), f32)

    def activated(at, width):
        z = ext[pl.ds(HALO - 3, TOK), at : at + width] * filt[0:1, at : at + width]
        for j in range(1, 4):
            z = z + ext[pl.ds(HALO - 3 + j, TOK), at : at + width] * filt[j : j + 1, at : at + width]
        return z * sigmoid(z)

    rows, cols = masks()
    inclusive = rows >= cols
    strict = rows > cols
    lower = jnp.where(inclusive, 1.0, 0.0).astype(bf16)
    eye = jnp.where(rows == cols, 1.0, 0.0)
    scal = bdv[...]
    c_all = mm(
        jnp.concatenate([lower, lower, lower], axis=1), jnp.concatenate(thirds(scal), axis=0)
    )
    kept_o[0:TOK, AT_C : AT_C + TOK] = c_all
    c_t = c_all.T
    b_t = scal.T
    heads = range(HEADS)
    qs, ks, vs, lows, invs, fadings = [], [], [], [], [], []
    for h in heads:
        a_q = activated(h * DK, DK)
        a_k = activated(QK + h * DK, DK)
        q = (
            a_q
            * lax.rsqrt(jnp.sum(a_q * a_q, axis=1, keepdims=True) + smallest)
            * DK ** (-0.5)
        ).astype(bf16)
        k = (a_k * lax.rsqrt(jnp.sum(a_k * a_k, axis=1, keepdims=True) + smallest)).astype(bf16)
        low_o[0:TOK, AT_Q + h * DK : AT_Q + (h + 1) * DK] = q
        low_o[0:TOK, AT_K + h * DK : AT_K + (h + 1) * DK] = k
        qs.append(q)
        ks.append(k)
        fading = fading_of(
            c_all[:, HEADS + h : HEADS + h + 1], c_t[HEADS + h : HEADS + h + 1, :], inclusive
        )
        fadings.append(fading)
        lows.append(jnp.where(strict, fading * b_t[h : h + 1, :] * mt(k, k), 0.0))
    pairs = (rows // 2 == cols // 2) & strict
    invs = [eye - jnp.where(pairs, low, 0.0) for low in lows]
    size = 2
    while size < TOK:
        part = (
            (rows // (2 * size) == cols // (2 * size))
            & (rows // size % 2 == 1)
            & (cols // size % 2 == 0)
        )
        steps = [mm3(jnp.where(part, lows[h], 0.0), invs[h]) for h in heads]
        invs = [invs[h] - mm3(invs[h], steps[h]) for h in heads]
        size *= 2
    vs = [activated(2 * QK + h * DV, DV).astype(bf16) for h in heads]
    u_vs = [mm2(invs[h], vs[h]) for h in heads]
    u_ks = [mm2(invs[h] * jnp.exp(c_t[HEADS + h : HEADS + h + 1, :]), ks[h]) for h in heads]
    for h in heads:
        u_v, u_k, q, k = u_vs[h], u_ks[h], qs[h], ks[h]
        c_col = c_all[:, HEADS + h : HEADS + h + 1]
        b_col = scal[:, h : h + 1]
        kept_o[0:TOK, AT_X + h * TOK : AT_X + (h + 1) * TOK] = invs[h]
        kept_o[0:TOK, h * DV : (h + 1) * DV] = u_v
        low_o[0:TOK, AT_U + h * DK : AT_U + (h + 1) * DK] = u_k.astype(bf16)
        scores = fadings[h] * mt(q, k) * b_t[h : h + 1, :]
        out_o[:, h * DV : (h + 1) * DV] = mm(scores, u_v)
        out_o[:, VW + h * DK : VW + (h + 1) * DK] = (
            jnp.exp(c_col) * q.astype(f32) - mm(scores, u_k)
        )
        c_last = c_all[TOK - 1 : TOK, HEADS + h : HEADS + h + 1]
        b_k = b_col * jnp.exp(c_last - c_col) * k.astype(f32)
        turned = (eye * jnp.exp(c_last) - tm(u_k, b_k)).astype(bf16)
        offset = tm(u_v, b_k).astype(bf16)
        for g in range(4):
            send_o[h * 4 + g, 0:DK] = turned
            send_o[h * 4 + g, DK : DK + 64] = offset[64 * g : 64 * g + 64]
    copies = [
        pltpu.make_async_copy(low_o, low_hbm, sems.at[0]),
        pltpu.make_async_copy(kept_o, kept_hbm, sems.at[1]),
    ]
    for copy in copies:
        copy.start()
    for copy in copies:
        copy.wait()


def scan_kernel(maps, out):
    state = jnp.zeros((64, DK), f32)
    for d in range(SEQ):
        out[d] = state.astype(bf16)
        if d < SEQ - 1:
            turned = maps[d, 0:DK]
            state = mm(
                jnp.concatenate(halves(state), axis=1), jnp.concatenate([turned, turned], axis=0)
            ) + maps[d, DK : DK + 64].astype(f32)


def scan_back_kernel(grads, maps, out):
    state = jnp.zeros((64, DK), f32)
    for d in range(SEQ - 1, -1, -1):
        out[d] = state.astype(bf16)
        if d > 0:
            turned = maps[d, 0:DK]
            state = mt(
                jnp.concatenate(halves(state), axis=1), jnp.concatenate([turned, turned], axis=1)
            ) + grads[d].astype(f32)


def mixed_kernel(out_hbm, st, gate_hbm, gain, mixed_o, gated_o, out, gate_pre, sems):
    finish_copies(fetch([(out_hbm, out), (gate_hbm, gate_pre)], sems))
    for h in range(HEADS):
        at = slice(h * DV, (h + 1) * DV)
        state = st[4 * h : 4 * h + 4].reshape(DV, DK)
        mixed = out[:, at] + mt(out[:, VW + h * DK : VW + (h + 1) * DK], state)
        mixed_o[:, at] = mixed
        normed = mixed * lax.rsqrt(jnp.mean(mixed * mixed, axis=1, keepdims=True) + epsilon)
        gate = gate_pre[:, at]
        gated_o[:, at] = (normed * gain[...] * (gate * sigmoid(gate))).astype(bf16)


def mixed_back_kernel(gated_grad, mixed_in, gate_pre, gain, out, do_o, gp_o, gain_o, sg_o):
    gain_total = jnp.zeros((1, DV), f32)
    for h in range(HEADS):
        at = slice(h * DV, (h + 1) * DV)
        mixed = mixed_in[:, at]
        root = lax.rsqrt(jnp.mean(mixed * mixed, axis=1, keepdims=True) + epsilon)
        m = mixed * root
        gate = gate_pre[:, at]
        sig = sigmoid(gate)
        grad = gated_grad[:, at]
        gm = grad * m
        silu = gate * sig
        gain_total = gain_total + jnp.sum(gm * silu, axis=0, keepdims=True)
        gp_o[:, at] = (gm * gain[...] * (sig * (1.0 + gate * (1.0 - sig)))).astype(bf16)
        e = grad * gain[...] * silu
        d_out = (root * (e - m * jnp.mean(e * m, axis=1, keepdims=True))).astype(bf16)
        do_o[:, at] = d_out
        sg = tm(d_out, out[:, VW + h * DK : VW + (h + 1) * DK])
        sg_o[4 * h : 4 * h + 4] = sg.astype(bf16).reshape(4, 64, DK)
    gain_o[...] = gain_total


def back_kernel(
    low_hbm, kept_hbm, do_hbm, st_hbm, gt_i, dz_o, dzh_o, fg_o, low_o, head_o,
    ext, low_i, kept_i, do_i, st_i, sems,
):
    copies = [
        pltpu.make_async_copy(source, target, sems.at[n])
        for n, (source, target) in enumerate(
            ((low_hbm, low_i), (kept_hbm, kept_i), (do_hbm, do_i), (st_hbm, st_i))
        )
    ]
    for copy in copies:
        copy.start()
    for copy in copies:
        copy.wait()
    ext[...] = low_i[:, 0:PRE].astype(f32)
    filt = kept_i[TOK:, :]
    rows, cols = masks()
    inclusive = rows >= cols
    strict = rows > cols
    scal = kept_i[0:TOK, AT_B : AT_B + TOK]
    c_all = kept_i[0:TOK, AT_C : AT_C + TOK]
    c_t = c_all.T
    b_t = scal.T

    def before_silu(at, width):
        z = ext[pl.ds(HALO - 3, TOK), at : at + width] * filt[0:1, at : at + width]
        for j in range(1, 4):
            z = z + ext[pl.ds(HALO - 3 + j, TOK), at : at + width] * filt[j : j + 1, at : at + width]
        return z

    def finish(grad, z, sig, at, width):
        dz = grad * (sig * (1.0 + z * (1.0 - sig)))
        dz_o[:, at : at + width] = dz
        dzh_o[:, at : at + width] = dz[0:HALO].astype(bf16)
        for j in range(4):
            fg_o[j : j + 1, at : at + width] = jnp.sum(
                dz * ext[pl.ds(HALO - 3 + j, TOK), at : at + width], axis=0, keepdims=True
            )

    fg_o[4:8, :] = jnp.zeros((4, PRE), f32)
    lane = lax.broadcasted_iota(jnp.int32, (TOK, TOK), 1)
    cols_acc = jnp.zeros((TOK, TOK), f32)
    sub = lax.broadcasted_iota(jnp.int32, (TOK, TOK), 0)
    rows_acc = jnp.zeros((TOK, TOK), f32)
    heads = range(HEADS)
    at_v = [slice(h * DV, (h + 1) * DV) for h in heads]
    q = [low_i[0:TOK, AT_Q + h * DK : AT_Q + (h + 1) * DK] for h in heads]
    k = [low_i[0:TOK, AT_K + h * DK : AT_K + (h + 1) * DK] for h in heads]
    st = [st_i[4 * h : 4 * h + 4].reshape(DV, DK) for h in heads]
    gt = [gt_i[4 * h : 4 * h + 4].reshape(DV, DK) for h in heads]
    c_col = [c_all[:, HEADS + h : HEADS + h + 1] for h in heads]
    c_row = [c_t[HEADS + h : HEADS + h + 1, :] for h in heads]
    c_last = [c_all[TOK - 1 : TOK, HEADS + h : HEADS + h + 1] for h in heads]
    b_col = [scal[:, h : h + 1] for h in heads]
    b_row = [b_t[h : h + 1, :] for h in heads]
    fading = [fading_of(c_col[h], c_row[h], inclusive) for h in heads]
    growth = [jnp.exp(c_col[h]) for h in heads]
    remains = [jnp.exp(c_last[h] - c_col[h]) for h in heads]
    scores = [fading[h] * mt(q[h], k[h]) for h in heads]
    low_one = [jnp.where(strict, fading[h] * mt(k[h], k[h]), 0.0) for h in heads]
    u = [
        kept_i[0:TOK, at_v[h]]
        - mt(low_i[0:TOK, AT_U + h * DK : AT_U + (h + 1) * DK], st[h])
        for h in heads
    ]
    w = [(b_col[h] * u[h]).astype(bf16) for h in heads]
    k_rem = [remains[h] * k[h].astype(f32) for h in heads]
    d_w = [tm(scores[h], do_i[:, at_v[h]]) + mt(k_rem[h], gt[h]) for h in heads]
    d_beta = [jnp.sum(u[h] * d_w[h], axis=1, keepdims=True) for h in heads]
    d_r = [
        tm(kept_i[0:TOK, AT_X + h * TOK : AT_X + (h + 1) * TOK], b_col[h] * d_w[h]) for h in heads
    ]
    d_rl = [d_r[h].astype(bf16) for h in heads]
    d_low = [jnp.where(strict, -mt(d_rl[h], u[h]), 0.0) for h in heads]
    d_a = [jnp.where(inclusive, mt(do_i[:, at_v[h]], w[h]), 0.0) for h in heads]
    d_qk = [d_a[h] * fading[h] for h in heads]
    e_beta = [d_low[h] * low_one[h] for h in heads]
    e_sum = [d_a[h] * scores[h] + e_beta[h] * b_row[h] for h in heads]
    d_kk = [d_low[h] * fading[h] * b_row[h] for h in heads]
    d_os = [mm(do_i[:, at_v[h]], st[h]) for h in heads]
    d_rs = [mm(d_rl[h], st[h]) for h in heads]
    w_g = [mm(w[h], gt[h]) for h in heads]
    dq = [mm(d_qk[h], k[h]) + growth[h] * d_os[h] for h in heads]
    dk = [
        tm(d_qk[h], q[h])
        + mm(d_kk[h], k[h])
        + tm(d_kk[h], k[h])
        - growth[h] * d_rs[h]
        + remains[h] * w_g[h]
        for h in heads
    ]
    for h in heads:
        rem_sum = jnp.sum(k_rem[h] * w_g[h], axis=1, keepdims=True)
        d_c = (
            jnp.sum(e_sum[h], axis=1, keepdims=True)
            + growth[h]
            * jnp.sum(
                q[h].astype(f32) * d_os[h] - k[h].astype(f32) * d_rs[h], axis=1, keepdims=True
            )
            - rem_sum
        )
        last = jnp.sum(rem_sum, axis=0, keepdims=True) + jnp.exp(c_last[h]) * jnp.sum(
            jnp.sum(st[h].astype(f32) * gt[h].astype(f32), axis=1, keepdims=True),
            axis=0,
            keepdims=True,
        )
        d_c = d_c + jnp.where(sub[:, 0:1] == TOK - 1, last, 0.0)
        cols_acc = cols_acc + jnp.where(lane == h, d_beta[h], 0.0)
        cols_acc = cols_acc + jnp.where(lane == HEADS + h, d_c, 0.0)
        rows_acc = rows_acc + jnp.where(sub == h, jnp.sum(e_beta[h], axis=0, keepdims=True), 0.0)
        rows_acc = rows_acc - jnp.where(
            sub == HEADS + h, jnp.sum(e_sum[h], axis=0, keepdims=True), 0.0
        )
    for h in heads:
        for grad, base, scale in ((dq[h], 0, DK ** (-0.5)), (dk[h], QK, 1.0)):
            at = base + h * DK
            z = before_silu(at, DK)
            sig = sigmoid(z)
            act = z * sig
            root = lax.rsqrt(jnp.sum(act * act, axis=1, keepdims=True) + smallest)
            unit = act * root
            grad = grad * scale
            d_act = root * (grad - unit * jnp.sum(unit * grad, axis=1, keepdims=True))
            finish(d_act, z, sig, at, DK)
        at = 2 * QK + h * DV
        z = before_silu(at, DV)
        finish(d_r[h], z, sigmoid(z), at, DV)
    total = cols_acc + rows_acc.T
    upper = jnp.where(rows <= cols, 1.0, 0.0).astype(bf16)
    summed = mm(
        jnp.concatenate([upper, upper, upper], axis=1), jnp.concatenate(thirds(total), axis=0)
    )
    grads = jnp.where(lane < HEADS, total, summed)
    sloped = grads * kept_i[0:TOK, AT_S : AT_S + TOK]
    low_o[...] = sloped.astype(bf16)
    head_o[0:1, :] = jnp.sum(grads * scal, axis=0, keepdims=True)
    head_o[1:2, :] = jnp.sum(sloped, axis=0, keepdims=True)
    head_o[2:8, :] = jnp.zeros((6, TOK), f32)


def conv_back_kernel(dz, after, filt, pre_o, ext):
    ext[0:TOK] = dz[...]
    ext[TOK:] = after[...].astype(f32)
    for at in range(0, PRE, 256):
        total = ext[pl.ds(3, TOK), at : at + 256] * filt[0:1, at : at + 256]
        for j in range(1, 4):
            total = total + ext[pl.ds(3 - j, TOK), at : at + 256] * filt[j : j + 1, at : at + 256]
        pre_o[:, at : at + 256] = total.astype(bf16)


def input_grad_kernel(part, part_in, middle_grad, inputs, gain_mix, grad_o):
    grad = part[...].astype(f32) + part_in[...].astype(f32)
    values = inputs[...].astype(f32)
    root = lax.rsqrt(jnp.mean(values * values, axis=1, keepdims=True) + epsilon)
    unit = values * root
    e = grad * gain_mix[...]
    grad_o[...] = (
        middle_grad[...] + root * (e - unit * jnp.mean(e * unit, axis=1, keepdims=True))
    ).astype(bf16)


def smalls_kernel(part, inputs, gain, ffn_gain_grad, normed, logits, taps, heads, small_o):
    values = inputs[...].astype(f32)
    root = lax.rsqrt(jnp.mean(values * values, axis=1, keepdims=True) + epsilon)
    mix_grad = jnp.sum(part[...].astype(f32) * (values * root), axis=0, keepdims=True)
    gain_grad = gain[...]
    logit_grads = tm(logits[...], normed[...])[0:8]
    log_grad = heads[0:1, HEADS : 2 * HEADS]
    bias_grad = heads[1:2, HEADS : 2 * HEADS]
    head = jnp.concatenate([log_grad, bias_grad], axis=1)
    high = head.astype(bf16).astype(f32)
    head = jnp.concatenate([high, head - high, jnp.zeros((1, 64 - 4 * HEADS), f32)], axis=1)
    ffn = ffn_gain_grad[...]
    tap = taps[0:4, :]
    for j in range(SEQ):
        wide = slice(64 * j, 64 * j + 64)
        small_o[j] = jnp.concatenate(
            [
                jnp.concatenate([mix_grad[:, wide], ffn[:, wide]], axis=1),
                jnp.concatenate(
                    [gain_grad[:, 16 * j : 16 * j + 16], jnp.zeros((1, 48), f32), head], axis=1
                ),
                jnp.zeros((2, 128), f32),
                jnp.concatenate([logit_grads[0:4, wide], logit_grads[4:8, wide]], axis=1),
                jnp.concatenate(
                    [
                        tap[:, 2 * QK + 64 * j : 2 * QK + 64 * j + 64],
                        tap[:, 32 * j : 32 * j + 32],
                        tap[:, QK + 32 * j : QK + 32 * j + 32],
                    ],
                    axis=1,
                ),
                jnp.zeros((4, 128), f32),
            ],
            axis=0,
        ).astype(bf16)


def padded_rows(left):
    return -(-(left.shape[1] // SEQ) // 16) * 16


def pieces_rows(pieces):
    return sum(padded_rows(left) * (right.shape[1] // 128) for left, right in pieces)


def weight_body(count, added, refs):
    ins = refs[: 2 * count]
    adds = refs[2 * count : 2 * count + added]
    out = refs[2 * count + added]
    turned = refs[2 * count + added + 1]
    offset = 0
    part = 0
    done = 0
    for at in range(count):
        left, right = ins[2 * at], ins[2 * at + 1]
        width = left.shape[1]
        rows = width // SEQ
        padded = padded_rows(left)
        turned[0:width] = left[...].T

        def tiles(n, count, right=right, width=width, rows=rows, padded=padded, offset=offset,
                  part=part, done=done):
            wide = jnp.dot(
                turned[0:width],
                right[:, pl.ds(pl.multiple_of(n * 128, 128), 128 * count)],
                preferred_element_type=f32,
            )
            for m in range(count):
                piece = wide[:, m * 128 : (m + 1) * 128].reshape(SEQ, rows, 128)
                if padded > rows:
                    piece = jnp.concatenate(
                        [piece, jnp.zeros((SEQ, padded - rows, 128), f32)], axis=1
                    )
                if part < added:
                    where = pl.ds(pl.multiple_of(offset - done + (n + m) * padded, 16), padded)
                    piece = piece + adds[part][:, where].astype(f32)
                where = pl.ds(pl.multiple_of(offset + (n + m) * padded, 16), padded)
                out[:, where] = piece.astype(bf16)

        def pair(n, carry, tiles=tiles):
            tiles(2 * n, 2)
            return carry

        count_here = right.shape[1] // 128
        lax.fori_loop(0, count_here // 2, pair, 0)
        if count_here % 2:
            tiles(count_here - 1, 1)
        offset += padded * (right.shape[1] // 128)
        if part < added and offset - done == adds[part].shape[1]:
            done = offset
            part += 1


def weight_grads(pieces, adds=()):
    total = pieces_rows(pieces)
    args = [operand for pair in pieces for operand in pair] + list(adds)

    def body(*refs):
        weight_body(len(pieces), len(adds), refs)

    return kernel_call(
        body,
        [((SEQ, total, 128), bf16)],
        *args,
        scratch=[pltpu.VMEM((1408, TOK), bf16)],
        spare=6 * MIB,
        flops=2 * 128 * 128 * SEQ * total,
        main=(0,),
    )[0]


def fetch(pairs, sems, first=0):
    copies = [
        pltpu.make_async_copy(source, target, sems.at[first + n])
        for n, (source, target) in enumerate(pairs)
    ]
    for copy in copies:
        copy.start()
    return copies


def finish_copies(copies):
    for copy in copies:
        copy.wait()


def late_body(place, normed, pre_kept, late_in, smalls, *refs):
    outs = refs[0:8]
    turned, kept, late_add, sems = refs[8:]
    rows = kept.shape[2] // 2
    fetched = fetch([(late_in, late_add)], sems)
    sent = []
    for s in range(4):
        x_to = lax.rem(place[1] + s, 4)
        sent += fetch([(smalls.at[:, x_to], outs[s].at[:, pl.ds(rows, 16)])], sems, 1 + s)
    turned[...] = normed[...].T
    finish_copies(fetched)
    for n in range(pre_kept.shape[1] // 256):
        wide = jnp.dot(
            turned[...], pre_kept[:, n * 256 : (n + 1) * 256], preferred_element_type=f32
        )
        for m in range(2):
            where = slice((2 * n + m) * 64, (2 * n + m + 1) * 64)
            piece = wide[:, m * 128 : (m + 1) * 128].reshape(SEQ, 64, 128)
            piece = piece + late_add[:, where].astype(f32)
            kept[:, :, where] = piece.astype(bf16).reshape(4, 4, 64, 128)
        if 2 * (n + 1) * 64 == rows:
            for s in range(4):
                x_to = lax.rem(place[1] + s, 4)
                sent += fetch(
                    [(kept.at[:, x_to, pl.ds(0, rows)], outs[s].at[:, pl.ds(0, rows)])], sems, 5 + s
                )
    for s in range(4):
        z_to = lax.rem(place[0] + s, 4)
        sent += fetch([(kept.at[z_to, :, pl.ds(rows, rows)], outs[4 + s])], sems, 9 + s)
    finish_copies(sent)


def in_order(terms, own):
    total = None
    for source in range(4):
        which = lax.rem(own + 4 - source, 4)
        term = jnp.zeros(terms[0].shape, f32)
        for n in range(4):
            term = jnp.where(which == n, terms[n].astype(f32), term)
        total = term if total is None else total + term
    return total


def plain_sum(terms):
    total = terms[0].astype(f32)
    for term in terms[1:]:
        total = total + term.astype(f32)
    return total


def sum_spread_body(place, *refs):
    outs, parts, sems = refs[8:16], refs[16:24], refs[24]
    finish_copies(fetch(zip(refs[0:8], parts), sems))
    first, second = parts[0:4], parts[4:8]
    rows = first[0].shape[1]
    for s in range(4):
        z_to = lax.rem(place[0] + s, 4)
        x_to = lax.rem(place[1] + s, 4)
        outs[s][...] = plain_sum([part[z_to] for part in first]).astype(bf16)
        outs[s][rows - 16 :] = in_order(
            [part[z_to, rows - 16 : rows] for part in first], place[1]
        ).astype(bf16)
        outs[4 + s][...] = plain_sum([part[x_to] for part in second]).astype(bf16)


def sum_body(place, *refs):
    out, parts, sems = refs[8], refs[9:17], refs[17]
    finish_copies(fetch(zip(refs[0:8], parts), sems))
    first, second = parts[0:4], parts[4:8]
    rows = first[0].shape[0]
    out[0:rows] = plain_sum([part[...] for part in first]).astype(bf16)
    out[rows - 16 : rows] = in_order(
        [part[rows - 16 : rows] for part in first], place[0]
    ).astype(bf16)
    out[rows:] = plain_sum([part[...] for part in second]).astype(bf16)


def fill(first, mine, other, out, core, at, rows=64, padded=64, count=None, first_tile=0):
    same = first if core == 0 else jnp.logical_not(first)
    for n in range(out.shape[1] // 128 if count is None else count):
        spot = slice(at + n * padded, at + n * padded + padded)
        block = jnp.where(same, mine[spot].astype(f32), other[spot].astype(f32))
        column = (first_tile + n) * 128
        out[:, column : column + 128] = block.astype(bf16)[0:rows]


def unpack_early_body(place, mine, other, gate_o, up_o, down_o, outgate_o, wout_o):
    put = functools.partial(fill, place[2] == 0, mine, other)
    put(gate_o, 0, 0)
    put(up_o, 1, 0)
    at = gate_o.shape[1] // 128 * 64
    tiles = down_o.shape[1] // 256
    put(down_o, 0, at, 88, 96, tiles)
    put(down_o, 1, at, 88, 96, tiles, tiles)
    at += 96 * tiles
    put(outgate_o, 0, at)
    put(wout_o, 1, at)


def unpack_late_body(
    place, mine, other, over_tensor, over_both, query_o, key_o, value_o, mix_o, ffn_o, gain_o,
    log_o, bias_o, beta_o, decay_o, taps_q_o, taps_k_o, taps_v_o,
):
    put = functools.partial(fill, place[2] == 0, mine, other)
    half = VW // 4
    put(query_o, 0, 0)
    put(key_o, 0, half + 16)
    put(value_o, 1, 0, count=4)
    put(value_o, 1, half + 16, count=4, first_tile=4)
    small = mine[half : half + 16].astype(f32) + other[half : half + 16].astype(f32)
    both = small[0:2] + (over_tensor[0:2].astype(f32) + over_both[0:2].astype(f32))
    mix_o[...] = both[0:1, 0:64].astype(bf16)
    ffn_o[...] = small[0:1, 64:128].astype(bf16)
    gain_o[...] = both[1:2, 0:16].astype(bf16)
    for n, out in enumerate((log_o, bias_o)):
        start = 64 + n * HEADS
        out[...] = (
            small[1:2, start : start + HEADS]
            + small[1:2, start + 2 * HEADS : start + 3 * HEADS]
        ).astype(bf16)
    beta_o[...] = small[4:8, 0:64].astype(bf16)
    decay_o[...] = small[4:8, 64:128].astype(bf16)
    taps_q_o[...] = small[8:12, 64:96].astype(bf16)
    taps_k_o[...] = small[8:12, 96:128].astype(bf16)
    taps_v_o[...] = small[8:12, 0:64].astype(bf16)


def placed_call(body, outs, place, *args, main=False, far=(), far_outs=(), scratch=(), limit=12):
    kind = pltpu.HBM if main else jax.ShapeDtypeStruct
    return pl.pallas_call(
        body,
        out_shape=[kind(shape, bf16) for shape in outs],
        in_specs=[pl.BlockSpec(memory_space=pltpu.SMEM)]
        + [
            pl.BlockSpec(memory_space=pltpu.HBM if n in far else pltpu.VMEM)
            for n in range(len(args))
        ],
        out_specs=[
            pl.BlockSpec(memory_space=pltpu.HBM if n in far_outs else pltpu.VMEM)
            for n in range(len(outs))
        ],
        scratch_shapes=list(scratch),
        compiler_params=pltpu.CompilerParams(vmem_limit_bytes=limit * MIB),
    )(place, *args)


def along_x(steps):
    return [(z * 4 + x, z * 4 + (x + steps) % 4) for z in range(4) for x in range(4)]


def along_z(steps):
    return [(z * 4 + x, (z + steps) % 4 * 4 + x) for z in range(4) for x in range(4)]


def swap_tensor(value):
    return lax.ppermute(value, "tensor", [(0, 1), (1, 0)])


def swap_core(value):
    return lax.ppermute(value, "dp", [(0, 1), (1, 0), (2, 3), (3, 2)])


def swap_both(value):
    pairs = [(t * 4 + d, (1 - t) * 4 + d // 2 * 2 + 1 - d % 2) for t in range(2) for d in range(4)]
    return lax.ppermute(value, ("tensor", "dp"), pairs)


def swap_far(value):
    return lax.ppermute(value, "dp", [(0, 2), (2, 0), (1, 3), (3, 1)])


def shift(value, steps):
    first, last = max(0, -steps), min(SEQ, SEQ - steps)
    return lax.ppermute(value, "seq", [(at, at + steps) for at in range(first, last)])


def exchange(value):
    return lax.all_to_all(value, "seq", 0, 0, tiled=True)


def dot(a, b):
    return jnp.dot(a, b, preferred_element_type=f32)


def dot_t(a, b):
    return lax.dot_general(a, b, (((1,), (1,)), ((), ())), preferred_element_type=f32)


def norm_parts(values):
    root = lax.rsqrt(jnp.mean(values * values, axis=-1, keepdims=True) + epsilon)
    return root, values * root


def norm_back(grad, gain, root, unit):
    e = grad * gain
    return root * (e - unit * jnp.mean(e * unit, axis=-1, keepdims=True))


def per_device(
    inputs,
    cotangent,
    norm_mix,
    w_query,
    w_key,
    w_value,
    w_outgate,
    w_beta,
    w_decay,
    decay_log,
    decay_bias,
    conv_query,
    conv_key,
    conv_value,
    out_gain,
    w_out,
    norm_ffn,
    w_gate,
    w_up,
    w_down,
):
    width = inputs.shape[2]
    first = lax.axis_index("dp") % 2 == 0
    at = lax.axis_index("seq")
    place = jnp.stack([at // 4, at % 4, lax.axis_index("dp") % 2]).astype(jnp.int32)
    residual = inputs.reshape(TOK, width).astype(f32)
    feed_grad = cotangent.reshape(TOK, width)
    gain_mix = norm_mix.astype(f32)
    gain_ffn = norm_ffn.astype(f32)
    gain_head = out_gain.astype(f32).reshape(1, DV)
    filters = jnp.concatenate([conv_query, conv_key, conv_value], axis=0).astype(f32)
    filt = jnp.pad(filters.T, ((0, 4), (0, 0)))

    root_mix, unit_mix = norm_parts(residual)
    normed_low = (unit_mix * gain_mix).astype(bf16)
    mixed_pre = jnp.concatenate(
        [dot(normed_low, w_query), dot(normed_low, w_key), dot(normed_low, w_value)], axis=1
    ).astype(bf16)
    halo = shift(mixed_pre[TOK - HALO :], 1)
    beta_rows = jax.nn.sigmoid(dot(normed_low, w_beta))
    decay_at = dot(normed_low, w_decay) + decay_bias.astype(f32)
    decay_rate = -jnp.exp(decay_log.astype(f32))
    decays = decay_rate * jax.nn.softplus(decay_at)

    def lanes(values, others):
        return jnp.pad(jnp.concatenate([values, others], axis=1), ((0, 0), (0, 120)))

    bdv = lanes(beta_rows, decays)
    slopes = lanes(beta_rows * (1.0 - beta_rows), decay_rate * jax.nn.sigmoid(decay_at))
    gate_pre = dot(normed_low, w_outgate)

    kept_low, kept, out_local, maps = kernel_call(
        front_kernel,
        [KEPT_LOW, KEPT, ((TOK, VW + QK), f32), ((SEQ, DK + 64, DK), bf16)],
        mixed_pre,
        halo,
        filt,
        bdv,
        slopes,
        scratch=[
            pltpu.VMEM((TOK + HALO, PRE), f32),
            pltpu.VMEM(*KEPT_LOW),
            pltpu.VMEM(*KEPT),
            pltpu.SemaphoreType.DMA((2,)),
        ],
        far_outs=(0, 1),
        main=(3,),
    )
    maps = exchange(maps)
    (states,) = kernel_call(scan_kernel, [((SEQ, 64, DK), bf16)], maps, main=(0,))
    states = exchange(states)
    mixed, gated_low = kernel_call(
        mixed_kernel,
        [((TOK, VW), f32), ((TOK, VW), bf16)],
        out_local,
        states,
        gate_pre,
        gain_head,
        scratch=[
            pltpu.VMEM((TOK, VW + QK), f32),
            pltpu.VMEM((TOK, VW), f32),
            pltpu.SemaphoreType.DMA((2,)),
        ],
        far=(0, 2),
    )
    branch = dot(gated_low, w_out).astype(bf16)
    branch_in = swap_tensor(branch)
    hidden_grad = dot_t(feed_grad, w_down)
    middle = residual + (branch.astype(f32) + branch_in.astype(f32))
    root_ffn, unit_ffn = norm_parts(middle)
    two_low = (unit_ffn * gain_ffn).astype(bf16)
    gate_ffn = dot(two_low, w_gate)
    up_ffn = dot(two_low, w_up)
    sig = jax.nn.sigmoid(gate_ffn)
    silu = gate_ffn * sig
    hidden_low = (silu * up_ffn).astype(bf16)
    gate_low = (hidden_grad * up_ffn * (sig * (1.0 + gate_ffn * (1.0 - sig)))).astype(bf16)
    up_low = (hidden_grad * silu).astype(bf16)
    half = width // 2
    ffn_sent = weight_grads(
        [
            (two_low, jnp.where(first, up_low, gate_low)),
            (hidden_low, jnp.where(first, feed_grad[:, half:], feed_grad[:, :half])),
        ]
    )
    ffn_in = swap_core(ffn_sent)
    ffn_sent, gate_next, up_next = lax.optimization_barrier((ffn_sent, gate_low, up_low))
    two_part = (dot_t(gate_next, w_gate) + dot_t(up_next, w_up)).astype(bf16)
    two_in = swap_tensor(two_part)

    two_grad = two_part.astype(f32) + two_in.astype(f32)
    grad_norm_ffn = jnp.sum(two_grad * unit_ffn, axis=0)
    middle_grad = feed_grad.astype(f32) + norm_back(two_grad, gain_ffn, root_ffn, unit_ffn)
    branch_low = middle_grad.astype(bf16)
    gated_grad = dot_t(branch_low, w_out)
    mixed_grad, gate_pre_low, gain_grad, start_grad = kernel_call(
        mixed_back_kernel,
        [((TOK, VW), bf16), ((TOK, VW), bf16), ((1, DV), f32), ((SEQ, 64, DK), bf16)],
        gated_grad,
        mixed,
        gate_pre,
        gain_head,
        out_local,
        main=(3,),
    )
    out_sent = weight_grads(
        [
            (
                jnp.where(first, gated_low, normed_low),
                jnp.where(first, branch_low, gate_pre_low),
            )
        ]
    )
    early = weight_grads(
        [
            (two_low, jnp.where(first, gate_low, up_low)),
            (hidden_low, jnp.where(first, feed_grad[:, :half], feed_grad[:, half:])),
            (
                jnp.where(first, normed_low, gated_low),
                jnp.where(first, gate_pre_low, branch_low),
            ),
        ],
        [ffn_in, swap_core(out_sent)],
    )
    start_grad, early = lax.optimization_barrier((exchange(start_grad), early))
    early = lax.optimization_barrier(
        lax.psum_scatter(early, "seq", scatter_dimension=0, tiled=True)
    )
    (end_grads,) = kernel_call(
        scan_back_kernel, [((SEQ, 64, DK), bf16)], start_grad, maps, main=(0,)
    )
    end_grads = exchange(end_grads)
    dz, dz_first, filter_grad, logit_low, head_grads = kernel_call(
        back_kernel,
        [
            ((TOK, PRE), f32),
            ((HALO, PRE), bf16),
            ((8, PRE), f32),
            ((TOK, TOK), bf16),
            ((8, TOK), f32),
        ],
        kept_low,
        kept,
        mixed_grad,
        states,
        end_grads,
        scratch=[
            pltpu.VMEM((TOK + HALO, PRE), f32),
            pltpu.VMEM(*KEPT_LOW),
            pltpu.VMEM(*KEPT),
            pltpu.VMEM((TOK, VW), bf16),
            pltpu.VMEM((SEQ, 64, DK), bf16),
            pltpu.SemaphoreType.DMA((4,)),
        ],
        far=(0, 1, 2, 3),
        main=(1,),
    )
    (pre_low,) = kernel_call(
        conv_back_kernel,
        [((TOK, PRE), bf16)],
        dz,
        shift(dz_first, -1),
        filt,
        scratch=[pltpu.VMEM((TOK + HALO, PRE), f32)],
    )
    part = (
        dot_t(pre_low[:, :QK], w_query)
        + dot_t(pre_low[:, QK : 2 * QK], w_key)
        + dot_t(pre_low[:, 2 * QK :], w_value)
        + dot_t(gate_pre_low, w_outgate)
        + dot_t(logit_low[:, :HEADS], w_beta)
        + dot_t(logit_low[:, HEADS : 2 * HEADS], w_decay)
    ).astype(bf16)
    late_sent = weight_grads(
        [(normed_low, jnp.where(first, pre_low[:, 2 * QK :], pre_low[:, : 2 * QK]))]
    )
    late_in = swap_core(late_sent)
    (smalls,) = kernel_call(
        smalls_kernel,
        [((SEQ, 16, 128), bf16)],
        part,
        inputs.reshape(TOK, width),
        gain_grad,
        grad_norm_ffn.reshape(1, width),
        normed_low,
        logit_low,
        filter_grad,
        head_grads,
    )
    half_rows = VW // 4
    small_rows = half_rows + 16
    blocks = placed_call(
        late_body,
        [(4, small_rows, 128)] * 4 + [(4, half_rows, 128)] * 4,
        place,
        normed_low,
        jnp.where(first, pre_low[:, : 2 * QK], pre_low[:, 2 * QK :]),
        late_in,
        smalls.reshape(4, 4, 16, 128),
        main=True,
        far=(2,),
        far_outs=range(8),
        scratch=[
            pltpu.VMEM((width, TOK), bf16),
            pltpu.VMEM((4, 4, 2 * half_rows, 128), bf16),
            pltpu.VMEM((SEQ, 2 * half_rows, 128), bf16),
            pltpu.SemaphoreType.DMA((13,)),
        ],
        limit=16,
    )
    moved = [blocks[0]] + [lax.ppermute(blocks[s], "seq", along_x(s)) for s in range(1, 4)]
    moved += [blocks[4]] + [lax.ppermute(blocks[4 + s], "seq", along_z(s)) for s in range(1, 4)]
    *_, part_next, hidden_last = lax.optimization_barrier((*blocks, part, hidden_low))
    feed_part = dot(hidden_last, w_down).astype(bf16)
    feed_in = swap_tensor(feed_part)
    output = (middle + (feed_part.astype(f32) + feed_in.astype(f32))).astype(bf16)
    part_in = swap_tensor(part_next)
    (grad_inputs,) = kernel_call(
        input_grad_kernel,
        [((TOK, width), bf16)],
        part_next,
        part_in,
        middle_grad,
        inputs.reshape(TOK, width),
        gain_mix.reshape(1, width),
    )
    *moved, grad_inputs, output = lax.optimization_barrier((*moved, grad_inputs, output))
    step_shapes = [(4, small_rows, 128)] * 4 + [(4, half_rows, 128)] * 4
    blocks = placed_call(
        sum_spread_body,
        [(small_rows, 128)] * 4 + [(half_rows, 128)] * 4,
        place,
        *moved,
        main=True,
        far=range(8),
        scratch=[pltpu.VMEM(shape, bf16) for shape in step_shapes]
        + [pltpu.SemaphoreType.DMA((8,))],
        limit=60,
    )
    moved = [blocks[0]] + [lax.ppermute(blocks[s], "seq", along_z(s)) for s in range(1, 4)]
    moved += [blocks[4]] + [lax.ppermute(blocks[4 + s], "seq", along_x(s)) for s in range(1, 4)]
    *moved, early = lax.optimization_barrier((*moved, early.reshape(-1, 128)))
    early_far = swap_far(early)
    (late,) = placed_call(
        sum_body,
        [(small_rows + half_rows, 128)],
        place,
        *moved,
        main=True,
        far=range(8),
        scratch=[pltpu.VMEM(shape[1:], bf16) for shape in step_shapes]
        + [pltpu.SemaphoreType.DMA((8,))],
        limit=60,
    )
    late_far, early, early_far = lax.optimization_barrier((swap_far(late), early, early_far))
    columns = w_gate.shape[1]
    early = (early.astype(f32) + early_far.astype(f32)).astype(bf16)
    grad_gate, grad_up, grad_down, grad_outgate, grad_wout = placed_call(
        unpack_early_body,
        [(64, columns), (64, columns), (88, width), (64, VW), (64, width)],
        place,
        early,
        swap_core(early),
    )
    late = (late.astype(f32) + late_far.astype(f32)).astype(bf16)
    small = late[half_rows:small_rows]
    shares = placed_call(
        unpack_late_body,
        [
            (64, QK),
            (64, QK),
            (64, VW),
            (1, 64),
            (1, 64),
            (1, 16),
            (1, HEADS),
            (1, HEADS),
            (4, 64),
            (4, 64),
            (4, 32),
            (4, 32),
            (4, 64),
        ],
        place,
        late,
        swap_core(late),
        swap_tensor(small),
        swap_both(small),
    )
    grad_query, grad_key, grad_value = shares[:3]
    mix, ffn, gain, log, bias, beta, decay, taps_q, taps_k, taps_v = shares[3:]
    return (
        output.reshape(inputs.shape),
        grad_inputs.reshape(inputs.shape),
        mix.reshape(-1),
        grad_query,
        grad_key,
        grad_value,
        grad_outgate,
        beta.T,
        decay.T,
        log.reshape(-1),
        bias.reshape(-1),
        taps_q.T,
        taps_k.T,
        taps_v.T,
        gain.reshape(-1),
        grad_wout,
        ffn.reshape(-1),
        grad_gate,
        grad_up,
        grad_down,
    )


def solution(mesh):
    return jax.shard_map(
        per_device,
        mesh=mesh,
        in_specs=(
            P("dp", "seq", None),
            P("dp", "seq", None),
            P(),
            P(None, "tensor"),
            P(None, "tensor"),
            P(None, "tensor"),
            P(None, "tensor"),
            P(None, "tensor"),
            P(None, "tensor"),
            P("tensor"),
            P("tensor"),
            P("tensor", None),
            P("tensor", None),
            P("tensor", None),
            P(),
            P("tensor", None),
            P(),
            P(None, "tensor"),
            P(None, "tensor"),
            P("tensor", None),
        ),
        out_specs=(
            P("dp", "seq", None),
            P("dp", "seq", None),
            P("seq"),
            P("seq", "tensor"),
            P("seq", "tensor"),
            P("seq", "tensor"),
            P("seq", "tensor"),
            P("seq", "tensor"),
            P("seq", "tensor"),
            P("tensor"),
            P("tensor"),
            P(("tensor", "seq"), None),
            P(("tensor", "seq"), None),
            P(("tensor", "seq"), None),
            P("seq"),
            P(("tensor", "seq"), None),
            P("seq"),
            P("seq", "tensor"),
            P("seq", "tensor"),
            P(("tensor", "seq"), None),
        ),
        check_vma=False,
    )
```

```python
import functools
import math

import jax
import jax.numpy as jnp
from jax import lax
from jax.experimental import pallas as pl
from jax.experimental.pallas import tpu as pltpu
from jax.sharding import PartitionSpec as P

f32 = jnp.float32
bf16 = jnp.bfloat16
epsilon = 1e-05
smallest = 1e-06
TOK = 128
HEADS = 4
DK = 128
DV = 256
QK = HEADS * DK
VW = HEADS * DV
PRE = 2 * QK + VW
SEQ = 16
HALO = 16
MIB = 1024 * 1024


def kernel_call(body, outs, *args, scratch=(), spare=4 * MIB, flops=0, far=(), far_outs=(), main=()):
    out_shape = [
        pltpu.HBM(shape, kind) if n in far_outs or n in main else jax.ShapeDtypeStruct(shape, kind)
        for n, (shape, kind) in enumerate(outs)
    ]
    moved = sum(a.size * a.dtype.itemsize for a in args)
    for shape, kind in outs:
        moved += math.prod(shape) * jnp.dtype(kind).itemsize
    limit = moved + spare
    return pl.pallas_call(
        body,
        out_shape=out_shape,
        in_specs=[
            pl.BlockSpec(memory_space=pltpu.HBM if n in far else pltpu.VMEM)
            for n in range(len(args))
        ],
        out_specs=[
            pl.BlockSpec(memory_space=pltpu.HBM if n in far_outs else pltpu.VMEM)
            for n in range(len(outs))
        ],
        scratch_shapes=list(scratch),
        compiler_params=pltpu.CompilerParams(vmem_limit_bytes=limit),
        cost_estimate=pl.CostEstimate(flops=flops, bytes_accessed=moved, transcendentals=0),
    )(*args)


def mm(a, b):
    return jnp.dot(a.astype(bf16), b.astype(bf16), preferred_element_type=f32)


def mt(a, b):
    return lax.dot_general(
        a.astype(bf16), b.astype(bf16), (((1,), (1,)), ((), ())), preferred_element_type=f32
    )


def tm(a, b):
    return lax.dot_general(
        a.astype(bf16), b.astype(bf16), (((0,), (0,)), ((), ())), preferred_element_type=f32
    )


def halves(a):
    high = a.astype(bf16)
    return high, (a - high.astype(f32)).astype(bf16)


def mm3(a, b):
    ah, al = halves(a)
    bh, bl = halves(b)
    return mm(jnp.concatenate([ah, al, ah], axis=1), jnp.concatenate([bh, bh, bl], axis=0))


def mm2(a, b):
    ah, al = halves(a)
    return mm(jnp.concatenate([ah, al], axis=1), jnp.concatenate([b, b], axis=0))


def thirds(a):
    high = a.astype(bf16)
    rest = a - high.astype(f32)
    mid = rest.astype(bf16)
    return high, mid, (rest - mid.astype(f32)).astype(bf16)


def masks():
    rows = lax.broadcasted_iota(jnp.int32, (TOK, TOK), 0)
    cols = lax.broadcasted_iota(jnp.int32, (TOK, TOK), 1)
    return rows, cols


def sigmoid(v):
    return 1.0 / (1.0 + jnp.exp(-v))


def fading_of(c_col, c_row, inclusive):
    return jnp.where(inclusive, jnp.exp(jnp.where(inclusive, c_col - c_row, 0.0)), 0.0)


AT_Q = PRE
AT_K = PRE + QK
AT_U = PRE + 2 * QK
KEPT_LOW = ((TOK + HALO, PRE + 3 * QK), bf16)
AT_X = VW
AT_C = VW + QK
AT_B = AT_C + TOK
AT_S = AT_B + TOK
KEPT = ((TOK + 8, PRE), f32)


def front_kernel(
    pre, halo, filt, bdv, slopes, low_hbm, kept_hbm, out_o, send_o, ext, low_o, kept_o, sems
):
    low_o[0:HALO, 0:PRE] = halo[...]
    low_o[HALO:, 0:PRE] = pre[...]
    low_o[TOK:, PRE:] = jnp.zeros((HALO, 3 * QK), bf16)
    ext[0:HALO] = halo[...].astype(f32)
    ext[HALO:] = pre[...].astype(f32)
    kept_o[TOK:, :] = filt[...]
    kept_o[0:TOK, AT_B : AT_B + TOK] = bdv[...]
    kept_o[0:TOK, AT_S : AT_S + TOK] = slopes[...]
    kept_o[0:TOK, AT_S + TOK :] = jnp.zeros((TOK, PRE - AT_S - TOK), f32)

    def activated(at, width):
        z = ext[pl.ds(HALO - 3, TOK), at : at + width] * filt[0:1, at : at + width]
        for j in range(1, 4):
            z = z + ext[pl.ds(HALO - 3 + j, TOK), at : at + width] * filt[j : j + 1, at : at + width]
        return z * sigmoid(z)

    rows, cols = masks()
    inclusive = rows >= cols
    strict = rows > cols
    lower = jnp.where(inclusive, 1.0, 0.0).astype(bf16)
    eye = jnp.where(rows == cols, 1.0, 0.0)
    scal = bdv[...]
    c_all = mm(
        jnp.concatenate([lower, lower, lower], axis=1), jnp.concatenate(thirds(scal), axis=0)
    )
    kept_o[0:TOK, AT_C : AT_C + TOK] = c_all
    c_t = c_all.T
    b_t = scal.T
    heads = range(HEADS)
    qs, ks, vs, lows, invs, fadings = [], [], [], [], [], []
    for h in heads:
        a_q = activated(h * DK, DK)
        a_k = activated(QK + h * DK, DK)
        q = (
            a_q
            * lax.rsqrt(jnp.sum(a_q * a_q, axis=1, keepdims=True) + smallest)
            * DK ** (-0.5)
        ).astype(bf16)
        k = (a_k * lax.rsqrt(jnp.sum(a_k * a_k, axis=1, keepdims=True) + smallest)).astype(bf16)
        low_o[0:TOK, AT_Q + h * DK : AT_Q + (h + 1) * DK] = q
        low_o[0:TOK, AT_K + h * DK : AT_K + (h + 1) * DK] = k
        qs.append(q)
        ks.append(k)
        fading = fading_of(
            c_all[:, HEADS + h : HEADS + h + 1], c_t[HEADS + h : HEADS + h + 1, :], inclusive
        )
        fadings.append(fading)
        lows.append(jnp.where(strict, fading * b_t[h : h + 1, :] * mt(k, k), 0.0))
    pairs = (rows // 2 == cols // 2) & strict
    invs = [eye - jnp.where(pairs, low, 0.0) for low in lows]
    size = 2
    while size < TOK:
        part = (
            (rows // (2 * size) == cols // (2 * size))
            & (rows // size % 2 == 1)
            & (cols // size % 2 == 0)
        )
        steps = [mm3(jnp.where(part, lows[h], 0.0), invs[h]) for h in heads]
        invs = [invs[h] - mm3(invs[h], steps[h]) for h in heads]
        size *= 2
    vs = [activated(2 * QK + h * DV, DV).astype(bf16) for h in heads]
    u_vs = [mm2(invs[h], vs[h]) for h in heads]
    u_ks = [mm2(invs[h] * jnp.exp(c_t[HEADS + h : HEADS + h + 1, :]), ks[h]) for h in heads]
    for h in heads:
        u_v, u_k, q, k = u_vs[h], u_ks[h], qs[h], ks[h]
        c_col = c_all[:, HEADS + h : HEADS + h + 1]
        b_col = scal[:, h : h + 1]
        kept_o[0:TOK, AT_X + h * TOK : AT_X + (h + 1) * TOK] = invs[h]
        kept_o[0:TOK, h * DV : (h + 1) * DV] = u_v
        low_o[0:TOK, AT_U + h * DK : AT_U + (h + 1) * DK] = u_k.astype(bf16)
        scores = fadings[h] * mt(q, k) * b_t[h : h + 1, :]
        out_o[:, h * DV : (h + 1) * DV] = mm(scores, u_v)
        out_o[:, VW + h * DK : VW + (h + 1) * DK] = (
            jnp.exp(c_col) * q.astype(f32) - mm(scores, u_k)
        )
        c_last = c_all[TOK - 1 : TOK, HEADS + h : HEADS + h + 1]
        b_k = b_col * jnp.exp(c_last - c_col) * k.astype(f32)
        turned = (eye * jnp.exp(c_last) - tm(u_k, b_k)).astype(bf16)
        offset = tm(u_v, b_k).astype(bf16)
        for g in range(4):
            send_o[h * 4 + g, 0:DK] = turned
            send_o[h * 4 + g, DK : DK + 64] = offset[64 * g : 64 * g + 64]
    copies = [
        pltpu.make_async_copy(low_o, low_hbm, sems.at[0]),
        pltpu.make_async_copy(kept_o, kept_hbm, sems.at[1]),
    ]
    for copy in copies:
        copy.start()
    for copy in copies:
        copy.wait()


def scan_kernel(maps, out):
    state = jnp.zeros((64, DK), f32)
    for d in range(SEQ):
        out[d] = state.astype(bf16)
        if d < SEQ - 1:
            turned = maps[d, 0:DK]
            state = mm(
                jnp.concatenate(halves(state), axis=1), jnp.concatenate([turned, turned], axis=0)
            ) + maps[d, DK : DK + 64].astype(f32)


def scan_back_kernel(grads, maps, out):
    state = jnp.zeros((64, DK), f32)
    for d in range(SEQ - 1, -1, -1):
        out[d] = state.astype(bf16)
        if d > 0:
            turned = maps[d, 0:DK]
            state = mt(
                jnp.concatenate(halves(state), axis=1), jnp.concatenate([turned, turned], axis=1)
            ) + grads[d].astype(f32)


def mixed_kernel(out_hbm, st, gate_hbm, gain, mixed_o, gated_o, out, gate_pre, sems):
    finish_copies(fetch([(out_hbm, out), (gate_hbm, gate_pre)], sems))
    for h in range(HEADS):
        at = slice(h * DV, (h + 1) * DV)
        state = st[4 * h : 4 * h + 4].reshape(DV, DK)
        mixed = out[:, at] + mt(out[:, VW + h * DK : VW + (h + 1) * DK], state)
        mixed_o[:, at] = mixed
        normed = mixed * lax.rsqrt(jnp.mean(mixed * mixed, axis=1, keepdims=True) + epsilon)
        gate = gate_pre[:, at]
        gated_o[:, at] = (normed * gain[...] * (gate * sigmoid(gate))).astype(bf16)


def mixed_back_kernel(gated_grad, mixed_in, gate_pre, gain, out, do_o, gp_o, gain_o, sg_o):
    gain_total = jnp.zeros((1, DV), f32)
    for h in range(HEADS):
        at = slice(h * DV, (h + 1) * DV)
        mixed = mixed_in[:, at]
        root = lax.rsqrt(jnp.mean(mixed * mixed, axis=1, keepdims=True) + epsilon)
        m = mixed * root
        gate = gate_pre[:, at]
        sig = sigmoid(gate)
        grad = gated_grad[:, at]
        gm = grad * m
        silu = gate * sig
        gain_total = gain_total + jnp.sum(gm * silu, axis=0, keepdims=True)
        gp_o[:, at] = (gm * gain[...] * (sig * (1.0 + gate * (1.0 - sig)))).astype(bf16)
        e = grad * gain[...] * silu
        d_out = (root * (e - m * jnp.mean(e * m, axis=1, keepdims=True))).astype(bf16)
        do_o[:, at] = d_out
        sg = tm(d_out, out[:, VW + h * DK : VW + (h + 1) * DK])
        sg_o[4 * h : 4 * h + 4] = sg.astype(bf16).reshape(4, 64, DK)
    gain_o[...] = gain_total


def back_kernel(
    low_hbm, kept_hbm, do_hbm, st_hbm, gt_i, dz_o, dzh_o, fg_o, low_o, head_o,
    ext, low_i, kept_i, do_i, st_i, sems,
):
    copies = [
        pltpu.make_async_copy(source, target, sems.at[n])
        for n, (source, target) in enumerate(
            ((low_hbm, low_i), (kept_hbm, kept_i), (do_hbm, do_i), (st_hbm, st_i))
        )
    ]
    for copy in copies:
        copy.start()
    for copy in copies:
        copy.wait()
    ext[...] = low_i[:, 0:PRE].astype(f32)
    filt = kept_i[TOK:, :]
    rows, cols = masks()
    inclusive = rows >= cols
    strict = rows > cols
    scal = kept_i[0:TOK, AT_B : AT_B + TOK]
    c_all = kept_i[0:TOK, AT_C : AT_C + TOK]
    c_t = c_all.T
    b_t = scal.T

    def before_silu(at, width):
        z = ext[pl.ds(HALO - 3, TOK), at : at + width] * filt[0:1, at : at + width]
        for j in range(1, 4):
            z = z + ext[pl.ds(HALO - 3 + j, TOK), at : at + width] * filt[j : j + 1, at : at + width]
        return z

    def finish(grad, z, sig, at, width):
        dz = grad * (sig * (1.0 + z * (1.0 - sig)))
        dz_o[:, at : at + width] = dz
        dzh_o[:, at : at + width] = dz[0:HALO].astype(bf16)
        for j in range(4):
            fg_o[j : j + 1, at : at + width] = jnp.sum(
                dz * ext[pl.ds(HALO - 3 + j, TOK), at : at + width], axis=0, keepdims=True
            )

    fg_o[4:8, :] = jnp.zeros((4, PRE), f32)
    lane = lax.broadcasted_iota(jnp.int32, (TOK, TOK), 1)
    cols_acc = jnp.zeros((TOK, TOK), f32)
    sub = lax.broadcasted_iota(jnp.int32, (TOK, TOK), 0)
    rows_acc = jnp.zeros((TOK, TOK), f32)
    heads = range(HEADS)
    at_v = [slice(h * DV, (h + 1) * DV) for h in heads]
    q = [low_i[0:TOK, AT_Q + h * DK : AT_Q + (h + 1) * DK] for h in heads]
    k = [low_i[0:TOK, AT_K + h * DK : AT_K + (h + 1) * DK] for h in heads]
    st = [st_i[4 * h : 4 * h + 4].reshape(DV, DK) for h in heads]
    gt = [gt_i[4 * h : 4 * h + 4].reshape(DV, DK) for h in heads]
    c_col = [c_all[:, HEADS + h : HEADS + h + 1] for h in heads]
    c_row = [c_t[HEADS + h : HEADS + h + 1, :] for h in heads]
    c_last = [c_all[TOK - 1 : TOK, HEADS + h : HEADS + h + 1] for h in heads]
    b_col = [scal[:, h : h + 1] for h in heads]
    b_row = [b_t[h : h + 1, :] for h in heads]
    fading = [fading_of(c_col[h], c_row[h], inclusive) for h in heads]
    growth = [jnp.exp(c_col[h]) for h in heads]
    remains = [jnp.exp(c_last[h] - c_col[h]) for h in heads]
    scores = [fading[h] * mt(q[h], k[h]) for h in heads]
    low_one = [jnp.where(strict, fading[h] * mt(k[h], k[h]), 0.0) for h in heads]
    u = [
        kept_i[0:TOK, at_v[h]]
        - mt(low_i[0:TOK, AT_U + h * DK : AT_U + (h + 1) * DK], st[h])
        for h in heads
    ]
    w = [(b_col[h] * u[h]).astype(bf16) for h in heads]
    k_rem = [remains[h] * k[h].astype(f32) for h in heads]
    d_w = [tm(scores[h], do_i[:, at_v[h]]) + mt(k_rem[h], gt[h]) for h in heads]
    d_beta = [jnp.sum(u[h] * d_w[h], axis=1, keepdims=True) for h in heads]
    d_r = [
        tm(kept_i[0:TOK, AT_X + h * TOK : AT_X + (h + 1) * TOK], b_col[h] * d_w[h]) for h in heads
    ]
    d_rl = [d_r[h].astype(bf16) for h in heads]
    d_low = [jnp.where(strict, -mt(d_rl[h], u[h]), 0.0) for h in heads]
    d_a = [jnp.where(inclusive, mt(do_i[:, at_v[h]], w[h]), 0.0) for h in heads]
    d_qk = [d_a[h] * fading[h] for h in heads]
    e_beta = [d_low[h] * low_one[h] for h in heads]
    e_sum = [d_a[h] * scores[h] + e_beta[h] * b_row[h] for h in heads]
    d_kk = [d_low[h] * fading[h] * b_row[h] for h in heads]
    d_os = [mm(do_i[:, at_v[h]], st[h]) for h in heads]
    d_rs = [mm(d_rl[h], st[h]) for h in heads]
    w_g = [mm(w[h], gt[h]) for h in heads]
    dq = [mm(d_qk[h], k[h]) + growth[h] * d_os[h] for h in heads]
    dk = [
        tm(d_qk[h], q[h])
        + mm(d_kk[h], k[h])
        + tm(d_kk[h], k[h])
        - growth[h] * d_rs[h]
        + remains[h] * w_g[h]
        for h in heads
    ]
    for h in heads:
        rem_sum = jnp.sum(k_rem[h] * w_g[h], axis=1, keepdims=True)
        d_c = (
            jnp.sum(e_sum[h], axis=1, keepdims=True)
            + growth[h]
            * jnp.sum(
                q[h].astype(f32) * d_os[h] - k[h].astype(f32) * d_rs[h], axis=1, keepdims=True
            )
            - rem_sum
        )
        last = jnp.sum(rem_sum, axis=0, keepdims=True) + jnp.exp(c_last[h]) * jnp.sum(
            jnp.sum(st[h].astype(f32) * gt[h].astype(f32), axis=1, keepdims=True),
            axis=0,
            keepdims=True,
        )
        d_c = d_c + jnp.where(sub[:, 0:1] == TOK - 1, last, 0.0)
        cols_acc = cols_acc + jnp.where(lane == h, d_beta[h], 0.0)
        cols_acc = cols_acc + jnp.where(lane == HEADS + h, d_c, 0.0)
        rows_acc = rows_acc + jnp.where(sub == h, jnp.sum(e_beta[h], axis=0, keepdims=True), 0.0)
        rows_acc = rows_acc - jnp.where(
            sub == HEADS + h, jnp.sum(e_sum[h], axis=0, keepdims=True), 0.0
        )
    for h in heads:
        for grad, base, scale in ((dq[h], 0, DK ** (-0.5)), (dk[h], QK, 1.0)):
            at = base + h * DK
            z = before_silu(at, DK)
            sig = sigmoid(z)
            act = z * sig
            root = lax.rsqrt(jnp.sum(act * act, axis=1, keepdims=True) + smallest)
            unit = act * root
            grad = grad * scale
            d_act = root * (grad - unit * jnp.sum(unit * grad, axis=1, keepdims=True))
            finish(d_act, z, sig, at, DK)
        at = 2 * QK + h * DV
        z = before_silu(at, DV)
        finish(d_r[h], z, sigmoid(z), at, DV)
    total = cols_acc + rows_acc.T
    upper = jnp.where(rows <= cols, 1.0, 0.0).astype(bf16)
    summed = mm(
        jnp.concatenate([upper, upper, upper], axis=1), jnp.concatenate(thirds(total), axis=0)
    )
    grads = jnp.where(lane < HEADS, total, summed)
    sloped = grads * kept_i[0:TOK, AT_S : AT_S + TOK]
    low_o[...] = sloped.astype(bf16)
    head_o[0:1, :] = jnp.sum(grads * scal, axis=0, keepdims=True)
    head_o[1:2, :] = jnp.sum(sloped, axis=0, keepdims=True)
    head_o[2:8, :] = jnp.zeros((6, TOK), f32)


def conv_back_kernel(dz, after, filt, pre_o, ext):
    ext[0:TOK] = dz[...]
    ext[TOK:] = after[...].astype(f32)
    for at in range(0, PRE, 256):
        total = ext[pl.ds(3, TOK), at : at + 256] * filt[0:1, at : at + 256]
        for j in range(1, 4):
            total = total + ext[pl.ds(3 - j, TOK), at : at + 256] * filt[j : j + 1, at : at + 256]
        pre_o[:, at : at + 256] = total.astype(bf16)


def input_grad_kernel(part, part_in, middle_grad, inputs, gain_mix, grad_o):
    grad = part[...].astype(f32) + part_in[...].astype(f32)
    values = inputs[...].astype(f32)
    root = lax.rsqrt(jnp.mean(values * values, axis=1, keepdims=True) + epsilon)
    unit = values * root
    e = grad * gain_mix[...]
    grad_o[...] = (
        middle_grad[...] + root * (e - unit * jnp.mean(e * unit, axis=1, keepdims=True))
    ).astype(bf16)


def smalls_kernel(part, inputs, gain, ffn_gain_grad, normed, logits, taps, heads, small_o):
    values = inputs[...].astype(f32)
    root = lax.rsqrt(jnp.mean(values * values, axis=1, keepdims=True) + epsilon)
    mix_grad = jnp.sum(part[...].astype(f32) * (values * root), axis=0, keepdims=True)
    gain_grad = gain[...]
    logit_grads = tm(logits[...], normed[...])[0:8]
    log_grad = heads[0:1, HEADS : 2 * HEADS]
    bias_grad = heads[1:2, HEADS : 2 * HEADS]
    head = jnp.concatenate([log_grad, bias_grad], axis=1)
    high = head.astype(bf16).astype(f32)
    head = jnp.concatenate([high, head - high, jnp.zeros((1, 64 - 4 * HEADS), f32)], axis=1)
    ffn = ffn_gain_grad[...]
    tap = taps[0:4, :]
    for j in range(SEQ):
        wide = slice(64 * j, 64 * j + 64)
        small_o[j] = jnp.concatenate(
            [
                jnp.concatenate([mix_grad[:, wide], ffn[:, wide]], axis=1),
                jnp.concatenate(
                    [gain_grad[:, 16 * j : 16 * j + 16], jnp.zeros((1, 48), f32), head], axis=1
                ),
                jnp.zeros((2, 128), f32),
                jnp.concatenate([logit_grads[0:4, wide], logit_grads[4:8, wide]], axis=1),
                jnp.concatenate(
                    [
                        tap[:, 2 * QK + 64 * j : 2 * QK + 64 * j + 64],
                        tap[:, 32 * j : 32 * j + 32],
                        tap[:, QK + 32 * j : QK + 32 * j + 32],
                    ],
                    axis=1,
                ),
                jnp.zeros((4, 128), f32),
            ],
            axis=0,
        ).astype(bf16)


def padded_rows(left):
    return -(-(left.shape[1] // SEQ) // 16) * 16


def pieces_rows(pieces):
    return sum(padded_rows(left) * (right.shape[1] // 128) for left, right in pieces)


def weight_body(count, added, refs):
    ins = refs[: 2 * count]
    adds = refs[2 * count : 2 * count + added]
    out = refs[2 * count + added]
    turned = refs[2 * count + added + 1]
    offset = 0
    part = 0
    done = 0
    for at in range(count):
        left, right = ins[2 * at], ins[2 * at + 1]
        width = left.shape[1]
        rows = width // SEQ
        padded = padded_rows(left)
        turned[0:width] = left[...].T

        def tiles(n, count, right=right, width=width, rows=rows, padded=padded, offset=offset,
                  part=part, done=done):
            wide = jnp.dot(
                turned[0:width],
                right[:, pl.ds(pl.multiple_of(n * 128, 128), 128 * count)],
                preferred_element_type=f32,
            )
            for m in range(count):
                piece = wide[:, m * 128 : (m + 1) * 128].reshape(SEQ, rows, 128)
                if padded > rows:
                    piece = jnp.concatenate(
                        [piece, jnp.zeros((SEQ, padded - rows, 128), f32)], axis=1
                    )
                if part < added:
                    where = pl.ds(pl.multiple_of(offset - done + (n + m) * padded, 16), padded)
                    piece = piece + adds[part][:, where].astype(f32)
                where = pl.ds(pl.multiple_of(offset + (n + m) * padded, 16), padded)
                out[:, where] = piece.astype(bf16)

        def pair(n, carry, tiles=tiles):
            tiles(2 * n, 2)
            return carry

        count_here = right.shape[1] // 128
        lax.fori_loop(0, count_here // 2, pair, 0)
        if count_here % 2:
            tiles(count_here - 1, 1)
        offset += padded * (right.shape[1] // 128)
        if part < added and offset - done == adds[part].shape[1]:
            done = offset
            part += 1


def weight_grads(pieces, adds=()):
    total = pieces_rows(pieces)
    args = [operand for pair in pieces for operand in pair] + list(adds)

    def body(*refs):
        weight_body(len(pieces), len(adds), refs)

    return kernel_call(
        body,
        [((SEQ, total, 128), bf16)],
        *args,
        scratch=[pltpu.VMEM((1408, TOK), bf16)],
        spare=6 * MIB,
        flops=2 * 128 * 128 * SEQ * total,
        main=(0,),
    )[0]


def fetch(pairs, sems, first=0):
    copies = [
        pltpu.make_async_copy(source, target, sems.at[first + n])
        for n, (source, target) in enumerate(pairs)
    ]
    for copy in copies:
        copy.start()
    return copies


def finish_copies(copies):
    for copy in copies:
        copy.wait()


def late_body(place, normed, pre_kept, late_in, smalls, *refs):
    outs = refs[0:8]
    turned, kept, late_add, sems = refs[8:]
    rows = kept.shape[2] // 2
    fetched = fetch([(late_in, late_add)], sems)
    sent = []
    for s in range(4):
        x_to = lax.rem(place[1] + s, 4)
        sent += fetch([(smalls.at[:, x_to], outs[s].at[:, pl.ds(rows, 16)])], sems, 1 + s)
    turned[...] = normed[...].T
    finish_copies(fetched)
    for n in range(pre_kept.shape[1] // 256):
        wide = jnp.dot(
            turned[...], pre_kept[:, n * 256 : (n + 1) * 256], preferred_element_type=f32
        )
        for m in range(2):
            where = slice((2 * n + m) * 64, (2 * n + m + 1) * 64)
            piece = wide[:, m * 128 : (m + 1) * 128].reshape(SEQ, 64, 128)
            piece = piece + late_add[:, where].astype(f32)
            kept[:, :, where] = piece.astype(bf16).reshape(4, 4, 64, 128)
        if 2 * (n + 1) * 64 == rows:
            for s in range(4):
                x_to = lax.rem(place[1] + s, 4)
                sent += fetch(
                    [(kept.at[:, x_to, pl.ds(0, rows)], outs[s].at[:, pl.ds(0, rows)])], sems, 5 + s
                )
    for s in range(4):
        z_to = lax.rem(place[0] + s, 4)
        sent += fetch([(kept.at[z_to, :, pl.ds(rows, rows)], outs[4 + s])], sems, 9 + s)
    finish_copies(sent)


def in_order(terms, own):
    total = None
    for source in range(4):
        which = lax.rem(own + 4 - source, 4)
        term = jnp.zeros(terms[0].shape, f32)
        for n in range(4):
            term = jnp.where(which == n, terms[n].astype(f32), term)
        total = term if total is None else total + term
    return total


def plain_sum(terms):
    total = terms[0].astype(f32)
    for term in terms[1:]:
        total = total + term.astype(f32)
    return total


def sum_spread_body(place, *refs):
    outs, parts, sems = refs[8:16], refs[16:24], refs[24]
    finish_copies(fetch(zip(refs[0:8], parts), sems))
    first, second = parts[0:4], parts[4:8]
    rows = first[0].shape[1]
    for s in range(4):
        z_to = lax.rem(place[0] + s, 4)
        x_to = lax.rem(place[1] + s, 4)
        outs[s][...] = plain_sum([part[z_to] for part in first]).astype(bf16)
        outs[s][rows - 16 :] = in_order(
            [part[z_to, rows - 16 : rows] for part in first], place[1]
        ).astype(bf16)
        outs[4 + s][...] = plain_sum([part[x_to] for part in second]).astype(bf16)


def sum_body(place, *refs):
    out, parts, sems = refs[8], refs[9:17], refs[17]
    finish_copies(fetch(zip(refs[0:8], parts), sems))
    first, second = parts[0:4], parts[4:8]
    rows = first[0].shape[0]
    out[0:rows] = plain_sum([part[...] for part in first]).astype(bf16)
    out[rows - 16 : rows] = in_order(
        [part[rows - 16 : rows] for part in first], place[0]
    ).astype(bf16)
    out[rows:] = plain_sum([part[...] for part in second]).astype(bf16)


def fill(first, mine, other, out, core, at, rows=64, padded=64, count=None, first_tile=0):
    same = first if core == 0 else jnp.logical_not(first)
    for n in range(out.shape[1] // 128 if count is None else count):
        spot = slice(at + n * padded, at + n * padded + padded)
        block = jnp.where(same, mine[spot].astype(f32), other[spot].astype(f32))
        column = (first_tile + n) * 128
        out[:, column : column + 128] = block.astype(bf16)[0:rows]


def unpack_body(place, mine, other, over_tensor, over_both, *outs):
    unpack_early(place, mine, other, VW // 2 + 16, *outs[:5])
    unpack_late(place, mine, other, over_tensor, over_both, *outs[5:])


def unpack_early(place, mine, other, at, gate_o, up_o, down_o, outgate_o, wout_o):
    put = functools.partial(fill, place[2] == 0, mine, other)
    put(gate_o, 0, at)
    put(up_o, 1, at)
    at += gate_o.shape[1] // 128 * 64
    tiles = down_o.shape[1] // 256
    put(down_o, 0, at, 88, 96, tiles)
    put(down_o, 1, at, 88, 96, tiles, tiles)
    at += 96 * tiles
    put(outgate_o, 0, at)
    put(wout_o, 1, at)


def unpack_late(
    place, mine, other, over_tensor, over_both, query_o, key_o, value_o, mix_o, ffn_o, gain_o,
    log_o, bias_o, beta_o, decay_o, taps_q_o, taps_k_o, taps_v_o,
):
    put = functools.partial(fill, place[2] == 0, mine, other)
    half = VW // 4
    put(query_o, 0, 0)
    put(key_o, 0, half + 16)
    put(value_o, 1, 0, count=4)
    put(value_o, 1, half + 16, count=4, first_tile=4)
    small = mine[half : half + 16].astype(f32) + other[half : half + 16].astype(f32)
    both = small[0:2] + (over_tensor[0:2].astype(f32) + over_both[0:2].astype(f32))
    mix_o[...] = both[0:1, 0:64].astype(bf16)
    ffn_o[...] = small[0:1, 64:128].astype(bf16)
    gain_o[...] = both[1:2, 0:16].astype(bf16)
    for n, out in enumerate((log_o, bias_o)):
        start = 64 + n * HEADS
        out[...] = (
            small[1:2, start : start + HEADS]
            + small[1:2, start + 2 * HEADS : start + 3 * HEADS]
        ).astype(bf16)
    beta_o[...] = small[4:8, 0:64].astype(bf16)
    decay_o[...] = small[4:8, 64:128].astype(bf16)
    taps_q_o[...] = small[8:12, 64:96].astype(bf16)
    taps_k_o[...] = small[8:12, 96:128].astype(bf16)
    taps_v_o[...] = small[8:12, 0:64].astype(bf16)


def placed_call(body, outs, place, *args, main=False, far=(), far_outs=(), scratch=(), limit=12):
    kind = pltpu.HBM if main else jax.ShapeDtypeStruct
    return pl.pallas_call(
        body,
        out_shape=[kind(shape, bf16) for shape in outs],
        in_specs=[pl.BlockSpec(memory_space=pltpu.SMEM)]
        + [
            pl.BlockSpec(memory_space=pltpu.HBM if n in far else pltpu.VMEM)
            for n in range(len(args))
        ],
        out_specs=[
            pl.BlockSpec(memory_space=pltpu.HBM if n in far_outs else pltpu.VMEM)
            for n in range(len(outs))
        ],
        scratch_shapes=list(scratch),
        compiler_params=pltpu.CompilerParams(vmem_limit_bytes=limit * MIB),
    )(place, *args)


def along_x(steps):
    return [(z * 4 + x, z * 4 + (x + steps) % 4) for z in range(4) for x in range(4)]


def along_z(steps):
    return [(z * 4 + x, (z + steps) % 4 * 4 + x) for z in range(4) for x in range(4)]


def swap_tensor(value):
    return lax.ppermute(value, "tensor", [(0, 1), (1, 0)])


def swap_core(value):
    return lax.ppermute(value, "dp", [(0, 1), (1, 0), (2, 3), (3, 2)])


def swap_both(value):
    pairs = [(t * 4 + d, (1 - t) * 4 + d // 2 * 2 + 1 - d % 2) for t in range(2) for d in range(4)]
    return lax.ppermute(value, ("tensor", "dp"), pairs)


def swap_far(value):
    return lax.ppermute(value, "dp", [(0, 2), (2, 0), (1, 3), (3, 1)])


def shift(value, steps):
    first, last = max(0, -steps), min(SEQ, SEQ - steps)
    return lax.ppermute(value, "seq", [(at, at + steps) for at in range(first, last)])


def exchange(value):
    return lax.all_to_all(value, "seq", 0, 0, tiled=True)


def dot(a, b):
    return jnp.dot(a, b, preferred_element_type=f32)


def dot_t(a, b):
    return lax.dot_general(a, b, (((1,), (1,)), ((), ())), preferred_element_type=f32)


def norm_parts(values):
    root = lax.rsqrt(jnp.mean(values * values, axis=-1, keepdims=True) + epsilon)
    return root, values * root


def norm_back(grad, gain, root, unit):
    e = grad * gain
    return root * (e - unit * jnp.mean(e * unit, axis=-1, keepdims=True))


def per_device(
    inputs,
    cotangent,
    norm_mix,
    w_query,
    w_key,
    w_value,
    w_outgate,
    w_beta,
    w_decay,
    decay_log,
    decay_bias,
    conv_query,
    conv_key,
    conv_value,
    out_gain,
    w_out,
    norm_ffn,
    w_gate,
    w_up,
    w_down,
):
    width = inputs.shape[2]
    first = lax.axis_index("dp") % 2 == 0
    at = lax.axis_index("seq")
    place = jnp.stack([at // 4, at % 4, lax.axis_index("dp") % 2]).astype(jnp.int32)
    residual = inputs.reshape(TOK, width).astype(f32)
    feed_grad = cotangent.reshape(TOK, width)
    gain_mix = norm_mix.astype(f32)
    gain_ffn = norm_ffn.astype(f32)
    gain_head = out_gain.astype(f32).reshape(1, DV)
    filters = jnp.concatenate([conv_query, conv_key, conv_value], axis=0).astype(f32)
    filt = jnp.pad(filters.T, ((0, 4), (0, 0)))

    root_mix, unit_mix = norm_parts(residual)
    normed_low = (unit_mix * gain_mix).astype(bf16)
    mixed_pre = jnp.concatenate(
        [dot(normed_low, w_query), dot(normed_low, w_key), dot(normed_low, w_value)], axis=1
    ).astype(bf16)
    halo = shift(mixed_pre[TOK - HALO :], 1)
    beta_rows = jax.nn.sigmoid(dot(normed_low, w_beta))
    decay_at = dot(normed_low, w_decay) + decay_bias.astype(f32)
    decay_rate = -jnp.exp(decay_log.astype(f32))
    decays = decay_rate * jax.nn.softplus(decay_at)

    def lanes(values, others):
        return jnp.pad(jnp.concatenate([values, others], axis=1), ((0, 0), (0, 120)))

    bdv = lanes(beta_rows, decays)
    slopes = lanes(beta_rows * (1.0 - beta_rows), decay_rate * jax.nn.sigmoid(decay_at))
    gate_pre = dot(normed_low, w_outgate)

    kept_low, kept, out_local, maps = kernel_call(
        front_kernel,
        [KEPT_LOW, KEPT, ((TOK, VW + QK), f32), ((SEQ, DK + 64, DK), bf16)],
        mixed_pre,
        halo,
        filt,
        bdv,
        slopes,
        scratch=[
            pltpu.VMEM((TOK + HALO, PRE), f32),
            pltpu.VMEM(*KEPT_LOW),
            pltpu.VMEM(*KEPT),
            pltpu.SemaphoreType.DMA((2,)),
        ],
        far_outs=(0, 1),
        main=(3,),
    )
    maps = exchange(maps)
    (states,) = kernel_call(scan_kernel, [((SEQ, 64, DK), bf16)], maps, main=(0,))
    states = exchange(states)
    mixed, gated_low = kernel_call(
        mixed_kernel,
        [((TOK, VW), f32), ((TOK, VW), bf16)],
        out_local,
        states,
        gate_pre,
        gain_head,
        scratch=[
            pltpu.VMEM((TOK, VW + QK), f32),
            pltpu.VMEM((TOK, VW), f32),
            pltpu.SemaphoreType.DMA((2,)),
        ],
        far=(0, 2),
    )
    branch = dot(gated_low, w_out).astype(bf16)
    branch_in = swap_tensor(branch)
    hidden_grad = dot_t(feed_grad, w_down)
    middle = residual + (branch.astype(f32) + branch_in.astype(f32))
    root_ffn, unit_ffn = norm_parts(middle)
    two_low = (unit_ffn * gain_ffn).astype(bf16)
    gate_ffn = dot(two_low, w_gate)
    up_ffn = dot(two_low, w_up)
    sig = jax.nn.sigmoid(gate_ffn)
    silu = gate_ffn * sig
    hidden_low = (silu * up_ffn).astype(bf16)
    gate_low = (hidden_grad * up_ffn * (sig * (1.0 + gate_ffn * (1.0 - sig)))).astype(bf16)
    up_low = (hidden_grad * silu).astype(bf16)
    half = width // 2
    ffn_sent = weight_grads(
        [
            (two_low, jnp.where(first, up_low, gate_low)),
            (hidden_low, jnp.where(first, feed_grad[:, half:], feed_grad[:, :half])),
        ]
    )
    ffn_in = swap_core(ffn_sent)
    ffn_sent, gate_next, up_next = lax.optimization_barrier((ffn_sent, gate_low, up_low))
    two_part = (dot_t(gate_next, w_gate) + dot_t(up_next, w_up)).astype(bf16)
    two_in = swap_tensor(two_part)

    two_grad = two_part.astype(f32) + two_in.astype(f32)
    grad_norm_ffn = jnp.sum(two_grad * unit_ffn, axis=0)
    middle_grad = feed_grad.astype(f32) + norm_back(two_grad, gain_ffn, root_ffn, unit_ffn)
    branch_low = middle_grad.astype(bf16)
    gated_grad = dot_t(branch_low, w_out)
    mixed_grad, gate_pre_low, gain_grad, start_grad = kernel_call(
        mixed_back_kernel,
        [((TOK, VW), bf16), ((TOK, VW), bf16), ((1, DV), f32), ((SEQ, 64, DK), bf16)],
        gated_grad,
        mixed,
        gate_pre,
        gain_head,
        out_local,
        main=(3,),
    )
    out_sent = weight_grads(
        [
            (
                jnp.where(first, gated_low, normed_low),
                jnp.where(first, branch_low, gate_pre_low),
            )
        ]
    )
    early = weight_grads(
        [
            (two_low, jnp.where(first, gate_low, up_low)),
            (hidden_low, jnp.where(first, feed_grad[:, :half], feed_grad[:, half:])),
            (
                jnp.where(first, normed_low, gated_low),
                jnp.where(first, gate_pre_low, branch_low),
            ),
        ],
        [ffn_in, swap_core(out_sent)],
    )
    start_grad, early = lax.optimization_barrier((exchange(start_grad), early))
    early = lax.optimization_barrier(
        lax.psum_scatter(early, "seq", scatter_dimension=0, tiled=True)
    )
    (end_grads,) = kernel_call(
        scan_back_kernel, [((SEQ, 64, DK), bf16)], start_grad, maps, main=(0,)
    )
    end_grads = exchange(end_grads)
    dz, dz_first, filter_grad, logit_low, head_grads = kernel_call(
        back_kernel,
        [
            ((TOK, PRE), f32),
            ((HALO, PRE), bf16),
            ((8, PRE), f32),
            ((TOK, TOK), bf16),
            ((8, TOK), f32),
        ],
        kept_low,
        kept,
        mixed_grad,
        states,
        end_grads,
        scratch=[
            pltpu.VMEM((TOK + HALO, PRE), f32),
            pltpu.VMEM(*KEPT_LOW),
            pltpu.VMEM(*KEPT),
            pltpu.VMEM((TOK, VW), bf16),
            pltpu.VMEM((SEQ, 64, DK), bf16),
            pltpu.SemaphoreType.DMA((4,)),
        ],
        far=(0, 1, 2, 3),
        main=(1,),
    )
    dz_after, gate_part = lax.optimization_barrier(
        (shift(dz_first, -1), dot_t(gate_pre_low, w_outgate))
    )
    (pre_low,) = kernel_call(
        conv_back_kernel,
        [((TOK, PRE), bf16)],
        dz,
        dz_after,
        filt,
        scratch=[pltpu.VMEM((TOK + HALO, PRE), f32)],
    )
    part = (
        dot_t(pre_low[:, :QK], w_query)
        + dot_t(pre_low[:, QK : 2 * QK], w_key)
        + dot_t(pre_low[:, 2 * QK :], w_value)
        + gate_part
        + dot_t(logit_low[:, :HEADS], w_beta)
        + dot_t(logit_low[:, HEADS : 2 * HEADS], w_decay)
    ).astype(bf16)
    late_sent = weight_grads(
        [(normed_low, jnp.where(first, pre_low[:, 2 * QK :], pre_low[:, : 2 * QK]))]
    )
    late_in = swap_core(late_sent)
    (smalls,) = kernel_call(
        smalls_kernel,
        [((SEQ, 16, 128), bf16)],
        part,
        inputs.reshape(TOK, width),
        gain_grad,
        grad_norm_ffn.reshape(1, width),
        normed_low,
        logit_low,
        filter_grad,
        head_grads,
    )
    half_rows = VW // 4
    small_rows = half_rows + 16
    blocks = placed_call(
        late_body,
        [(4, small_rows, 128)] * 4 + [(4, half_rows, 128)] * 4,
        place,
        normed_low,
        jnp.where(first, pre_low[:, : 2 * QK], pre_low[:, 2 * QK :]),
        late_in,
        smalls.reshape(4, 4, 16, 128),
        main=True,
        far=(2,),
        far_outs=range(8),
        scratch=[
            pltpu.VMEM((width, TOK), bf16),
            pltpu.VMEM((4, 4, 2 * half_rows, 128), bf16),
            pltpu.VMEM((SEQ, 2 * half_rows, 128), bf16),
            pltpu.SemaphoreType.DMA((13,)),
        ],
        limit=16,
    )
    moved = [blocks[0]] + [lax.ppermute(blocks[s], "seq", along_x(s)) for s in range(1, 4)]
    moved += [blocks[4]] + [lax.ppermute(blocks[4 + s], "seq", along_z(s)) for s in range(1, 4)]
    *_, part_next, hidden_last = lax.optimization_barrier((*blocks, part, hidden_low))
    feed_part = dot(hidden_last, w_down).astype(bf16)
    feed_in = swap_tensor(feed_part)
    output = (middle + (feed_part.astype(f32) + feed_in.astype(f32))).astype(bf16)
    part_in = swap_tensor(part_next)
    (grad_inputs,) = kernel_call(
        input_grad_kernel,
        [((TOK, width), bf16)],
        part_next,
        part_in,
        middle_grad,
        inputs.reshape(TOK, width),
        gain_mix.reshape(1, width),
    )
    *moved, grad_inputs, output = lax.optimization_barrier((*moved, grad_inputs, output))
    step_shapes = [(4, small_rows, 128)] * 4 + [(4, half_rows, 128)] * 4
    blocks = placed_call(
        sum_spread_body,
        [(small_rows, 128)] * 4 + [(half_rows, 128)] * 4,
        place,
        *moved,
        main=True,
        far=range(8),
        scratch=[pltpu.VMEM(shape, bf16) for shape in step_shapes]
        + [pltpu.SemaphoreType.DMA((8,))],
        limit=60,
    )
    moved = [blocks[0]] + [lax.ppermute(blocks[s], "seq", along_z(s)) for s in range(1, 4)]
    moved += [blocks[4]] + [lax.ppermute(blocks[4 + s], "seq", along_x(s)) for s in range(1, 4)]
    *moved, early = lax.optimization_barrier((*moved, early.reshape(-1, 128)))
    early_far = swap_far(early)
    (late,) = placed_call(
        sum_body,
        [(small_rows + half_rows, 128)],
        place,
        *moved,
        main=True,
        far=range(8),
        scratch=[pltpu.VMEM(shape[1:], bf16) for shape in step_shapes]
        + [pltpu.SemaphoreType.DMA((8,))],
        limit=60,
    )
    late_far, early, early_far = lax.optimization_barrier((swap_far(late), early, early_far))
    columns = w_gate.shape[1]
    mine = jnp.concatenate(
        [late.astype(f32) + late_far.astype(f32), early.astype(f32) + early_far.astype(f32)], axis=0
    ).astype(bf16)
    small = mine[half_rows:small_rows]
    shares = placed_call(
        unpack_body,
        [
            (64, columns),
            (64, columns),
            (88, width),
            (64, VW),
            (64, width),
            (64, QK),
            (64, QK),
            (64, VW),
            (1, 64),
            (1, 64),
            (1, 16),
            (1, HEADS),
            (1, HEADS),
            (4, 64),
            (4, 64),
            (4, 32),
            (4, 32),
            (4, 64),
        ],
        place,
        mine,
        swap_core(mine),
        swap_tensor(small),
        swap_both(small),
    )
    grad_gate, grad_up, grad_down, grad_outgate, grad_wout = shares[:5]
    shares = shares[5:]
    grad_query, grad_key, grad_value = shares[:3]
    mix, ffn, gain, log, bias, beta, decay, taps_q, taps_k, taps_v = shares[3:]
    return (
        output.reshape(inputs.shape),
        grad_inputs.reshape(inputs.shape),
        mix.reshape(-1),
        grad_query,
        grad_key,
        grad_value,
        grad_outgate,
        beta.T,
        decay.T,
        log.reshape(-1),
        bias.reshape(-1),
        taps_q.T,
        taps_k.T,
        taps_v.T,
        gain.reshape(-1),
        grad_wout,
        ffn.reshape(-1),
        grad_gate,
        grad_up,
        grad_down,
    )


def solution(mesh):
    return jax.shard_map(
        per_device,
        mesh=mesh,
        in_specs=(
            P("dp", "seq", None),
            P("dp", "seq", None),
            P(),
            P(None, "tensor"),
            P(None, "tensor"),
            P(None, "tensor"),
            P(None, "tensor"),
            P(None, "tensor"),
            P(None, "tensor"),
            P("tensor"),
            P("tensor"),
            P("tensor", None),
            P("tensor", None),
            P("tensor", None),
            P(),
            P("tensor", None),
            P(),
            P(None, "tensor"),
            P(None, "tensor"),
            P("tensor", None),
        ),
        out_specs=(
            P("dp", "seq", None),
            P("dp", "seq", None),
            P("seq"),
            P("seq", "tensor"),
            P("seq", "tensor"),
            P("seq", "tensor"),
            P("seq", "tensor"),
            P("seq", "tensor"),
            P("seq", "tensor"),
            P("tensor"),
            P("tensor"),
            P(("tensor", "seq"), None),
            P(("tensor", "seq"), None),
            P(("tensor", "seq"), None),
            P("seq"),
            P(("tensor", "seq"), None),
            P("seq"),
            P("seq", "tensor"),
            P("seq", "tensor"),
            P(("tensor", "seq"), None),
        ),
        check_vma=False,
    )
```
